128 devices in a mesh: dp: 2 (over y_lo), sp: 64 (over z, y_hi, x, core).
Axes of the slice: x: 4, y: 4 (y_hi: 2, y_lo: 2; y = y_hi * 2 + y_lo), z: 4, core: 2. Of those that a mesh axis runs over, the one named last changes fastest.
Arguments:
- acts: bfloat16 [6, 12288, 384], P(None, ('dp', 'sp')), may hold values from -6 to 6
- cotangent: bfloat16 [6, 12288, 384], P(None, ('dp', 'sp')), may hold values from -24 to 24
- lengths: int32 [6, 16], replicated, may hold values from 672 to 768
- w_qkv: bfloat16 [2, 384, 1152], P(None, ('dp', 'sp')), may hold values from -0.3125 to 0.3125
- w_out: bfloat16 [2, 384, 384], P(None, ('dp', 'sp')), may hold values from -6 to 6
- w_up: bfloat16 [2, 384, 1536], P(None, ('dp', 'sp')), may hold values from -0.3125 to 0.3125
- w_down: bfloat16 [2, 384, 1536], P(None, ('dp', 'sp')), may hold values from -0.15625 to 0.15625
- gains: bfloat16 [2, 384, 2], P(None, ('dp', 'sp')), may hold values from 0.099609375 to 1.8984375
- biases: bfloat16 [2, 384, 6], P(None, ('dp', 'sp')), may hold values from -3 to 3
- hidden_bias: bfloat16 [2, 1536], P(None, 'dp'), may hold values from -3 to 3
Outputs:
- activations: float32 [6, 12288, 384], P(None, ('dp', 'sp'))
- input_grad: float32 [6, 12288, 384], P(None, ('dp', 'sp'))
- grad_w_qkv: float32 [2, 384, 1152], P(None, ('dp', 'sp'))
- grad_w_out: float32 [2, 384, 384], P(None, ('dp', 'sp'))
- grad_w_up: float32 [2, 384, 1536], P(None, ('dp', 'sp'))
- grad_w_down: float32 [2, 384, 1536], P(None, ('dp', 'sp'))
- grad_gains: float32 [2, 384, 2], P(None, ('dp', 'sp'))
- grad_biases: float32 [2, 384, 6], P(None, ('dp', 'sp'))
- grad_hidden_bias: float32 [2, 1536], P(None, 'dp')
The draws below stay inside these ranges and needn't reach their ends.
Inputs may be any that keep to these rules, and one draw needn't show every extreme that they name: `lengths`: an image's valid tokens are its first ones; its other rows are padding.
All inputs are finite; a program needn't handle non-finite values.
Results may differ from the reference program's by a relative error of at most 0.011.
Values may be sent and summed in bfloat16 or wider, within the bound.
A program may use at most 256 MiB of HBM per device.

```python
import jax
import jax.numpy as jnp
from jax import lax

D = 384
HEADS = 6
HEAD_DIM = 64
FF = 1536
LAYERS = 2
MICRO = 6
IMG_TOK = 768
GROUPS = 16
ROWS = 12288
IMAGES = 96


def plant(entries, rng, least, top_value):
    place = [jax.random.randint(jax.random.fold_in(rng, axis), (), 0, length) for axis, length in enumerate(entries.shape)]
    main_axis = entries.shape.index(max(entries.shape))
    neighbour = place[:main_axis] + [(place[main_axis] + 1) % entries.shape[main_axis]] + place[main_axis + 1:]
    return entries.at[tuple(place)].set(least).at[tuple(neighbour)].set(top_value)


def spiked(values, key, source, target, shards_of, factor):
    def block_of(dim):
        return (jnp.arange(values.shape[dim]) // (values.shape[dim] // shards_of)).reshape((-1,) + (1,) * (values.ndim - 1 - dim))

    near = jax.random.permutation(key, shards_of)[block_of(target)]
    far = (block_of(target) + shards_of // 2) % shards_of
    return jnp.where((block_of(source) == near) | (block_of(source) == far), factor * values, values)


def levels(rng, dims, shards, low, top_value):
    gain = 1.0
    for dim, parts in shards:
        steps = jax.random.uniform(jax.random.fold_in(jax.random.fold_in(rng, 6), dim), (parts,), jnp.float32, low / len(shards), top_value / len(shards))
        gain = gain * jnp.repeat(jnp.exp(steps), dims[dim] // parts).reshape((-1,) + (1,) * (len(dims) - 1 - dim))
    return gain


def gaussian(key, extent, scale, limit, cuts=(), held_as=jnp.bfloat16):
    loudness = levels(key, extent, cuts, -0.22, 0.18) if cuts else 1.0
    drawn = jax.random.normal(key, extent, jnp.float32) * scale * loudness
    return jnp.minimum(jnp.maximum(drawn, -limit), limit).astype(held_as)


def noise_with(stream_key, extent, width, most, split, heavy, kind=jnp.bfloat16):
    drawn = width * jax.random.normal(stream_key, extent, jnp.float32)
    if split:
        drawn = drawn * levels(stream_key, extent, split, -0.22, 0.18)
    return jnp.clip(spiked(drawn, jax.random.fold_in(stream_key, 3), *heavy), -most, most).astype(kind)


def setup_inputs(seed: int = 0) -> dict:
    splits = jax.random.split(jax.random.key(seed), 11)
    return {
        "acts": gaussian(splits[0], (MICRO, ROWS, D), 1.0, 6.0, ((1, 128),)),
        "cotangent": noise_with(splits[1], (MICRO, ROWS, D), 1.0, 24.0, ((1, 128),), (1, 2, 128, 5.5)),
        "lengths": plant(jax.random.randint(splits[2], (MICRO, GROUPS), IMG_TOK - IMG_TOK // 8, IMG_TOK + 1), jax.random.fold_in(splits[2], 1), IMG_TOK - IMG_TOK // 8, IMG_TOK).astype(jnp.int32),
        "w_qkv": gaussian(splits[3], (LAYERS, D, 3 * D), D ** -0.5, 0.3125, ((1, 128),)),
        "w_out": gaussian(splits[4], (LAYERS, D, D), (max(D * 3 // IMG_TOK, 1)) ** -0.5, 6.0, ((1, 128),)),
        "w_up": gaussian(splits[5], (LAYERS, D, FF), D ** -0.5, 0.3125, ((1, 128),)),
        "w_down": gaussian(splits[6], (LAYERS, D, FF), FF ** -0.5, 0.15625, ((1, 128),)),
        "gains": jnp.clip(1.0 + 0.18 * jax.random.normal(splits[7], (LAYERS, D, 2), jnp.float32), 0.099609375, 1.8984375).astype(jnp.bfloat16),
        "biases": gaussian(splits[8], (LAYERS, D, 6), 0.5, 3.0, ((1, 128),)),
        "hidden_bias": gaussian(splits[9], (LAYERS, FF), 0.5, 3.0, ((1, 2),)),
    }


EPSILON = 1e-06
NEG_FILL = -1e+30

@jax.custom_vjp
def low(v):
    return lax.optimization_barrier(v.astype(jnp.bfloat16)).astype(jnp.float32)

@jax.custom_vjp
def low_back(v):
    return v

def low_keep(v):
    return (low(v), None)

def low_pass(kept, grad):
    return (grad,)

def back_keep(v):
    return (v, None)

def back_low(kept, grad):
    return (low(grad),)
low.defvjp(low_keep, low_pass)
low_back.defvjp(back_keep, back_low)

def matmul(left_side, right_side):
    return jnp.dot(left_side, right_side, precision=lax.Precision.HIGHEST, preferred_element_type=jnp.float32)

def layer_norm(values, gain_vec, shift_vec):
    center = values - lax.optimization_barrier(jnp.mean(values, axis=-1, keepdims=True))
    spread = lax.optimization_barrier(jnp.mean(center * center, axis=-1, keepdims=True))
    return center * lax.rsqrt(spread + EPSILON) * gain_vec + shift_vec

def attend_image(operands):
    queries, key_rows, value_rows, length = operands
    scores = jnp.einsum('qhd,khd->hqk', queries, key_rows, precision=lax.Precision.HIGHEST) * HEAD_DIM ** (-0.5)
    scores = low_back(scores)
    key_valid = jnp.arange(IMG_TOK, dtype=jnp.int32) < length
    scores = jnp.where(key_valid[None, None, :], scores, NEG_FILL)
    row_max = lax.optimization_barrier(jnp.max(scores, axis=-1, keepdims=True))
    exponent = jnp.exp(scores - row_max)
    probabilities = exponent / lax.optimization_barrier(jnp.sum(exponent, axis=-1, keepdims=True))
    return jnp.einsum('hqk,khd->qhd', low(probabilities), value_rows, precision=lax.Precision.HIGHEST)

def block_forward(residual, params, lengths):
    w_qkv, w_out, w_up, w_down, gains, biases, hidden_bias = params
    image_count = residual.shape[0]
    flat_rows = residual.reshape(-1, D)
    for layer_index in range(LAYERS):
        gain_cols = gains[layer_index]
        shift_cols = biases[layer_index]
        normed = low(layer_norm(flat_rows, gain_cols[:, 0], shift_cols[:, 3]))
        qkv_bias = jnp.concatenate([shift_cols[:, 0], jnp.zeros((D,), jnp.float32), shift_cols[:, 1]])
        mixed_qkv = low(low_back(matmul(normed, w_qkv[layer_index]) + qkv_bias))
        split_qkv = mixed_qkv.reshape(image_count, IMG_TOK, 3, HEADS, HEAD_DIM)
        attended = lax.map(jax.checkpoint(attend_image), (split_qkv[:, :, 0], split_qkv[:, :, 1], split_qkv[:, :, 2], lengths))
        attended = low(low_back(attended.reshape(-1, D)))
        flat_rows = flat_rows + low_back(matmul(attended, w_out[layer_index]) + shift_cols[:, 2])
        normed = low(layer_norm(flat_rows, gain_cols[:, 1], shift_cols[:, 4]))
        hidden = low_back(matmul(normed, w_up[layer_index]) + hidden_bias[layer_index])
        active = low(jax.nn.gelu(hidden, approximate=True))
        flat_rows = flat_rows + low_back(matmul(active, w_down[layer_index].T) + shift_cols[:, 5])
    return flat_rows.reshape(image_count, IMG_TOK, D)

def reference(acts, cotangent, lengths, w_qkv, w_out, w_up, w_down, gains, biases, hidden_bias):
    params = tuple((element.astype(jnp.float32) for element in (w_qkv, w_out, w_up, w_down, gains, biases, hidden_bias)))
    per_step = max((divisor for divisor in range(1, max(4096 // IMG_TOK, 1) + 1) if IMAGES % divisor == 0))
    step_count = IMAGES // per_step
    inputs = acts.astype(jnp.float32).reshape(step_count, per_step, IMG_TOK, D)
    cotan_rows = cotangent.astype(jnp.float32).reshape(step_count, per_step, IMG_TOK, D)
    counts = lengths.reshape(step_count, per_step)

    def accumulate(totals, batch_item):
        residual, upstream, length_rows = batch_item

        def forward(residual_in, *weights):
            return block_forward(residual_in, weights, length_rows)
        result, pull_back = jax.vjp(forward, residual, *params)
        grad_list = pull_back(upstream)
        updated = tuple((running + increment for running, increment in zip(totals, grad_list[1:])))
        return (updated, (result, grad_list[0]))
    zero_totals = tuple((jnp.zeros_like(element) for element in params))
    totals, (results, input_grads) = lax.scan(accumulate, zero_totals, (inputs, cotan_rows, counts))
    return (results.reshape(MICRO, ROWS, D), input_grads.reshape(MICRO, ROWS, D), totals[0], totals[1], totals[2], totals[3], totals[4], totals[5], totals[6])
```

```python
import math

import jax
import jax.numpy as jnp
from jax import lax
from jax.experimental import pallas as pl
from jax.experimental.pallas import tpu as pltpu
from jax.sharding import PartitionSpec as P

D = 384
HEADS = 6
PAIRS = HEADS // 2
HEAD_DIM = 64
FF = 1536
LAYERS = 2
TOK = 768
EPSILON = 1e-06
NEG_FILL = -1e30
GELU_COEF = math.sqrt(2.0 / math.pi)
CUBIC_COEF = 0.044715
BF = jnp.bfloat16
F32 = jnp.float32
RB = 384
FC = 512
MIB = 1024 * 1024

MISC0, OUT0, UP0, DOWN0, WIDE = 1152, 1280, 1664, 3200, 4864
UNITS = (
    (0, 0, 640, 384, (0, 32)),
    (0, 1280, 896, 384, (32, 64)),
    (0, 3072, 896, 384, (64, 96)),
    (1, 0, 640, 384, (0, 32)),
    (1, 1280, 1792, 896, (32, 96)),
)
COUNT = len(UNITS)
SLAB = 96
GROUPS = ((0, 0, 32), (0, 32, 96), (1, 0, 96))

OWNERS = (0, 1, 2, 4, 5, 6)
MESH = pl.DeviceIdType.MESH
SPLIT = 16
ROWS = 48


def dot(left_side, right_side):
    return jnp.dot(left_side, right_side, preferred_element_type=F32)


def dot_nt(left_side, right_side):
    return lax.dot_general(
        left_side, right_side, (((1,), (1,)), ((), ())), preferred_element_type=F32
    )


def dot_tn(left_side, right_side):
    return lax.dot_general(
        left_side, right_side, (((0,), (0,)), ((), ())), preferred_element_type=F32
    )


def normalized(values):
    center = values - jnp.mean(values, axis=-1, keepdims=True)
    inverse = lax.rsqrt(jnp.mean(center * center, axis=-1, keepdims=True) + EPSILON)
    return center * inverse, inverse


def norm_backward(upstream, xhat, inverse, gain):
    scaled = upstream * gain
    return inverse * (
        scaled
        - jnp.mean(scaled, axis=-1, keepdims=True)
        - xhat * jnp.mean(scaled * xhat, axis=-1, keepdims=True)
    )


def gelu_pair(hidden):
    square = hidden * hidden
    tangent = jnp.tanh(hidden * (GELU_COEF + (GELU_COEF * CUBIC_COEF) * square))
    half = 0.5 + 0.5 * tangent
    active = hidden * half
    slope = half + active * (1.0 - tangent) * (
        GELU_COEF + (3.0 * GELU_COEF * CUBIC_COEF) * square
    )
    return active, slope


def colsum(values):
    return jnp.sum(values.astype(F32), axis=0, keepdims=True)


def each_block(body):
    for start in range(0, TOK, RB):
        body(slice(start, start + RB))


def each_chunk(stop, width, body):
    for start in range(0, stop, width):
        body(slice(start, start + width), lambda base, at=start: slice(base + at, base + at + width))


def encoder(
    length, w, carry, inputs, cot, act, igrad, hid, hid_sums, row_sums,
    mids, qkv, probs_even, probs_odd, invs, att, att_low, active, slope, low_a, low_b, dqkv, trans, trans_b, prm,
):
    last_valid = lax.broadcasted_iota(jnp.int32, (1, 128), 1) + (TOK - 128) < length
    lanes = lax.broadcasted_iota(jnp.int32, (1, 128), 1)
    first_half = lanes < 64
    scale = HEAD_DIM ** (-0.5)

    def lanes_at(pair, base):
        return pl.ds(pl.multiple_of(base + 128 * pair, 128), 128)

    def half_of(block, which):
        keep = first_half if which == 0 else jnp.logical_not(first_half)
        return jnp.where(keep, block, jnp.zeros_like(block))

    def row(layer, index):
        at = (index + 6) % 8
        return prm[layer, at : at + 1, :]

    def project(layer):
        prm[layer] = w[layer, :, MISC0 : MISC0 + 128].astype(F32).T[0:8]

        bias = jnp.concatenate([row(layer, 2), jnp.zeros((1, D), F32), row(layer, 3)], axis=1)

        def body(rows):
            source = carry[rows, :]
            inputs[layer, rows, :] = source
            xhat, _inverse = normalized(source)
            low = (xhat * row(layer, 0) + row(layer, 5)).astype(BF)
            qkv[layer, rows, :] = (dot(low, w[layer, :, 0 : 3 * D]) + bias).astype(BF)

        each_block(body)
        trans[...] = qkv[layer, :, D : 2 * D].T

    def attend(layer, pair):
        lane = lanes_at(pair, 0)
        value = qkv[layer, :, lanes_at(pair, 2 * D)]
        value = jnp.concatenate([value, jnp.ones((TOK, 128), BF)], axis=1)

        def body(rows):
            query = qkv[layer, rows, lane] * jnp.asarray(scale, BF)
            results = []
            kept = invs[rows, :]
            for which in range(2):
                head = 2 * pair + which
                scores = dot(half_of(query, which), trans[lane, :])
                last = jnp.where(last_valid, scores[:, TOK - 128 :], NEG_FILL)
                scores = jnp.concatenate([scores[:, : TOK - 128], last], axis=1)
                low = jnp.exp(scores - jnp.max(scores, axis=-1, keepdims=True)).astype(BF)
                (probs_even, probs_odd)[which][layer, pair, rows, :] = low
                product = dot(low, value)
                inverse = 1.0 / product[:, 128:]
                results.append(product[:, :128] * inverse)
                kept = jnp.where(lanes == 8 * layer + head, inverse, kept)
            invs[rows, :] = kept
            whole = jnp.where(first_half, results[0], results[1])
            high = whole.astype(BF)
            att[layer, rows, lane] = high
            att_low[layer, rows, lane] = (whole - high.astype(F32)).astype(BF)

        each_block(body)

    def feed(layer):
        def body(rows):
            mid = inputs[layer, rows, :] + (
                dot(att[layer, rows, :], w[layer, :, OUT0 : OUT0 + D]) + row(layer, 4)
            )
            mids[layer, rows, :] = mid
            xhat, _inverse = normalized(mid)
            low = (xhat * row(layer, 1) + row(layer, 6)).astype(BF)
            total = mid + row(layer, 7)
            for chunk in range(FF // FC):
                cols = slice(FC * chunk, FC * chunk + FC)
                hidden = dot(low, w[layer, :, UP0 + FC * chunk : UP0 + FC * chunk + FC])
                value, rate = gelu_pair(hidden + hid[layer, :, cols])
                value = value.astype(BF)
                active[layer, rows, cols] = value
                slope[layer, rows, cols] = rate.astype(BF)
                total = total + dot_nt(
                    value, w[layer, :, DOWN0 + FC * chunk : DOWN0 + FC * chunk + FC]
                )
            carry[rows, :] = total
            act[rows, :] = total.astype(BF)

        each_block(body)

    def add_sum(layer, index, values):
        row_sums[layer, index : index + 1, :] += colsum(values)

    def turn_back():
        carry[...] = cot[...].astype(F32)

    def unfeed(layer):
        def body(rows):
            upstream = carry[rows, :]
            down = upstream.astype(BF)
            low_a[rows, :] = down
            add_sum(layer, 7, down)
            xhat, inverse = normalized(mids[layer, rows, :])
            low_b[rows, :] = (xhat * row(layer, 1) + row(layer, 6)).astype(BF)
            total = jnp.zeros((RB, D), F32)
            for chunk in range(FF // FC):
                cols = slice(FC * chunk, FC * chunk + FC)
                grad = dot(down, w[layer, :, DOWN0 + FC * chunk : DOWN0 + FC * chunk + FC])
                grad = (grad * slope[layer, rows, cols].astype(F32)).astype(BF)
                slope[layer, rows, cols] = grad
                hid_sums[layer, chunk : chunk + 1, :] += colsum(grad)
                total = total + dot_nt(grad, w[layer, :, UP0 + FC * chunk : UP0 + FC * chunk + FC])
            add_sum(layer, 1, total * xhat)
            add_sum(layer, 6, total)
            carry[rows, :] = upstream + norm_backward(total, xhat, inverse, row(layer, 1))

        each_block(body)

    def feed_grads(layer):
        trans[...] = low_a[...].T
        trans_b[...] = low_b[...].T

        def grad_down(cols, at):
            w[layer, :, at(DOWN0)] = dot(trans[...], active[layer, :, cols]).astype(BF)

        def grad_up(cols, at):
            w[layer, :, at(UP0)] = dot(trans_b[...], slope[layer, :, cols]).astype(BF)

        each_chunk(FF, FC, grad_down)
        each_chunk(FF, FC, grad_up)

    def unproject_out(layer):
        def body(rows):
            low = carry[rows, :].astype(BF)
            low_a[rows, :] = low
            add_sum(layer, 4, low)
            grad = dot_nt(low, w[layer, :, OUT0 : OUT0 + D])
            inverse = jnp.where(layer == 0, invs[rows, 0:8], invs[rows, 8:16])
            for pair in range(PAIRS):
                lane = slice(128 * pair, 128 * pair + 128)
                both = jnp.where(
                    first_half,
                    inverse[:, 2 * pair : 2 * pair + 1],
                    inverse[:, 2 * pair + 1 : 2 * pair + 2],
                )
                low_b[rows, lane] = (grad[:, lane] * both).astype(BF)

        each_block(body)
        trans[...] = att[layer].T
        w[layer, :, OUT0 : OUT0 + D] = dot(trans[...], low_a[...]).astype(BF)
        trans[...] = low_b[...].T
        trans_b[...] = (qkv[layer, :, 0:D] * jnp.asarray(scale, BF)).T

    def unattend(layer, pair):
        lane = lanes_at(pair, 0)
        key = qkv[layer, :, lanes_at(pair, D)]
        value = qkv[layer, :, lanes_at(pair, 2 * D)]
        key_parts, value_parts = [0.0, 0.0], [0.0, 0.0]

        def body(rows):
            grad = low_b[rows, lane]
            whole = att[layer, rows, lane].astype(F32) + att_low[layer, rows, lane].astype(F32)
            weighted = grad.astype(F32) * whole
            results = []
            for which, probs in enumerate((probs_even, probs_odd)):
                feature = pl.ds(pl.multiple_of(128 * pair + 64 * which, 64), 64)
                low = probs[layer, pair, rows, :]
                inner = jnp.sum(half_of(weighted, which), axis=-1, keepdims=True)
                prob_grad = dot_nt(half_of(grad, which), value)
                score_grad = (low.astype(F32) * (prob_grad - inner)).astype(BF)
                results.append(dot(score_grad, key))
                key_parts[which] += dot(trans_b[feature, rows], score_grad)
                value_parts[which] += dot(trans[feature, rows], low)
            dqkv[rows, lane] = (jnp.where(first_half, results[0], results[1]) * scale).astype(BF)

        each_block(body)
        dqkv[:, lanes_at(pair, D)] = jnp.concatenate(key_parts, axis=0).T.astype(BF)
        dqkv[:, lanes_at(pair, 2 * D)] = jnp.concatenate(value_parts, axis=0).T.astype(BF)

    def qkv_grads(layer):
        def body(rows):
            xhat, _inverse = normalized(inputs[layer, rows, :])
            low_a[rows, :] = (xhat * row(layer, 0) + row(layer, 5)).astype(BF)

        each_block(body)
        trans[...] = low_a[...].T

        def grad_qkv(cols, _at):
            active[layer, 0:D, cols] = dot(trans[...], dqkv[:, cols]).astype(BF)

        each_chunk(3 * D, D, grad_qkv)

    def unproject(layer, between):
        def body(rows):
            if rows.stop == TOK:
                between()
            add_sum(layer, 2, dqkv[rows, 0:D])
            add_sum(layer, 3, dqkv[rows, 2 * D : 3 * D])
            xhat, inverse = normalized(inputs[layer, rows, :])
            total = dot_nt(dqkv[rows, :], w[layer, :, 0 : 3 * D])
            add_sum(layer, 0, total * xhat)
            add_sum(layer, 5, total)
            upstream = carry[rows, :] + norm_backward(total, xhat, inverse, row(layer, 0))
            carry[rows, :] = upstream
            igrad[rows, :] = upstream.astype(BF)

        each_block(body)

    return (
        project, attend, feed, turn_back, unfeed, feed_grads, unproject_out, unattend, qkv_grads, unproject,
    )


def compute_scratch():
    return [
        pltpu.VMEM((LAYERS, TOK, D), F32),
        pltpu.VMEM((LAYERS, TOK, 3 * D), BF),
        pltpu.VMEM((LAYERS, PAIRS, TOK, TOK), BF),
        pltpu.VMEM((LAYERS, PAIRS, TOK, TOK), BF),
        pltpu.VMEM((TOK, 128), F32),
        pltpu.VMEM((LAYERS, TOK, D), BF),
        pltpu.VMEM((LAYERS, TOK, D), BF),
        pltpu.VMEM((LAYERS, TOK, FF), BF),
        pltpu.VMEM((LAYERS, TOK, FF), BF),
        pltpu.VMEM((TOK, D), BF),
        pltpu.VMEM((TOK, 3 * D), BF),
        pltpu.VMEM((D, TOK), BF),
        pltpu.VMEM((D, TOK), BF),
        pltpu.VMEM((LAYERS, 8, D), F32),
    ]


def device(dp, z, y, x, core):
    return (dp, z * 16 + y * 8 + x * 2 + core)


def turned(value, by, count):
    return lax.rem(value + (by + count), count)


def rows_at(block):
    return pl.ds(pl.multiple_of(block * ROWS, 16), ROWS)


def image_rows(position):
    return pl.ds(pl.multiple_of(position * 96, 16), 96)


def copy_to(source, target, send, recv, where):
    return pltpu.make_async_remote_copy(
        src_ref=source,
        dst_ref=target,
        send_sem=send,
        recv_sem=recv,
        device_id=where,
        device_id_type=MESH,
    )


def spread_matrix():
    out = lax.broadcasted_iota(jnp.int32, (4 * ROWS, 256), 0)
    col = lax.broadcasted_iota(jnp.int32, (4 * ROWS, 256), 1)
    member, inner, row = col >> 4, (col >> 2) & 3, col & 3
    hit = jnp.logical_and(out == ROWS * inner + 3 * member + row, row < 3)
    return jnp.where(hit, 1.0, 0.0).astype(BF)


def kernel(
    lengths, acts, cot_in, p_qkv, p_out, p_up, p_down, p_gains, p_biases, p_hid,
    o_qkv, o_out, o_up, o_down, o_gains, o_biases, o_hid, act_out, igrad_out,
    w, carry, inputs, img, cot, act, onehot, slab_build, hid_all, hid, hid_sums, row_sums, early, late, tall_sums,
    mids, qkv, probs_even, probs_odd, invs, att, att_low, active, slope, low_b, dqkv, trans, trans_b, prm,
    give, held, slabs, ends,
    h_core, h_y, h_z, h_p, h_sum, l_plane, l_far, l_sum,
    ga_send, ga_recv, gz_send, gz_recv, gy_send, gy_recv, gs_send, gs_recv,
    i_send, i_recv, i_local, b_send, b_recv,
    rc_send, rc_recv, ry_send, ry_recv, rz_send, rz_recv, rp_send, rp_recv,
    e_send, e_recv, e_local, h_send, h_recv, l_send, l_recv,
    *buffers,
):
    core_buf, y_buf, z_buf = [buffers[COUNT * kind : COUNT * kind + COUNT] for kind in range(3)]
    dp, sp = lax.axis_index("dp"), lax.axis_index("sp")
    z = lax.div(sp, 16)
    y = lax.rem(lax.div(sp, 8), 2)
    x = lax.rem(lax.div(sp, 2), 4)
    core = lax.rem(sp, 2)
    mine = y * 8 + x * 2 + core
    position = x * 2 + core
    entry_mine = position - lax.div(position, 4)
    owner = lax.rem(position, 4) < 3
    sibling = device(dp, z, y, x, 1 - core)
    igrad = img
    low_a = cot
    gathers, reduces = [], []

    def push(source, target, send, recv, where):
        copy_to(source, target, send, recv, where).start()

    def all_sent(steps):
        for view, sem, index in steps:
            ref, sem = view(), sem.at[index]
            copy_to(ref, ref, sem, sem, sibling).wait_send()

    def sent(steps, view, sem, *index):
        steps.append((view, sem, index))

    def arrived(ref, send, recv):
        copy_to(ref, ref, send, recv, sibling).wait_recv()

    peers = [sibling]
    for step in range(1, 4):
        peers.append(device(dp, z, y, turned(x, step, 4), core))
        peers.append(device(dp, z, y, turned(x, step, 4), 1 - core))
        peers.append(device(dp, turned(z, step, 4), y, x, core))
        peers.append(device(1 - dp, turned(z, step, 4), y, x, core))
    for step in range(4):
        peers.append(device(dp, z, 1 - y, turned(x, step, 4), core))
        peers.append(device(dp, z, 1 - y, turned(x, step, 4), 1 - core))
    for side in (y, 1 - y):
        peers.append(device(1 - dp, z, side, x, core))
    barrier = pltpu.get_barrier_semaphore()
    for peer in peers:
        pl.semaphore_signal(barrier, inc=1, device_id=peer, device_id_type=MESH)

    def misc_rows(layer):
        slab_build[0:8, :] = jnp.zeros((8, 128), F32)
        slab_build[0:3, 0:6] = p_biases[...].astype(F32)[:, layer, :]
        rows = slab_build[0:3, :]
        at = lax.broadcasted_iota(jnp.int32, (3, 128), 0)
        lane = lax.broadcasted_iota(jnp.int32, (3, 128), 1)
        gains = p_gains[...].astype(F32)
        for gain in range(2):
            for feature in range(3):
                hit = jnp.logical_and(at == feature, lane == 6 + gain)
                rows = jnp.where(hit, gains[layer, gain : gain + 1, feature : feature + 1], rows)
        return rows

    def slab_build_layer(layer):
        whole = jnp.concatenate(
            [p_qkv[...].astype(F32)[:, layer, :], misc_rows(layer)]
            + [ref[...].astype(F32)[:, layer, :] for ref in (p_out, p_up, p_down)]
            + [jnp.zeros((3, 128), F32)],
            axis=1,
        )
        for side in range(2):
            slab_build[...] = jnp.zeros_like(slab_build)
            for of, start, width, _first, rows in UNITS:
                for chunk in range(width // 128) if of == layer else ():
                    at = start + side * width + 128 * chunk
                    row = rows[0] + 4 * chunk
                    slab_build[row : row + 3, :] = whole[:, at : at + 128]
            give[layer, side] = slab_build[...].astype(BF)

    slab_build_layer(0)
    pl.semaphore_wait(barrier, len(peers))

    def plane_target(turn):
        return turned(y, turn // 8, 2), turned(x, turn // 2 % 4, 4), turned(core, turn % 2, 2)

    def plane_source(turn):
        return (
            turned(y, -(turn // 8), 2) * 8
            + turned(x, -(turn // 2 % 4), 4) * 2
            + turned(core, -(turn % 2), 2)
        )

    def slab_send(group):
        layer, begin, end = GROUPS[group]
        held[layer, mine, begin:end, :] = give[layer, core, begin:end, :]
        for turn in range(1, 16):
            to_y, to_x, to_core = plane_target(turn)
            push(
                give.at[layer, to_core, begin:end, :],
                held.at[layer, mine, begin:end, :],
                ga_send.at[group],
                ga_recv.at[group],
                device(dp, z, to_y, to_x, to_core),
            )
        sent(gathers, lambda: held.at[layer, 1:16, begin:end, :], ga_send, group)

    def slab_arrive(group):
        layer, begin, end = GROUPS[group]
        arrived(held.at[layer, 1:16, begin:end, :], ga_send.at[group], ga_recv.at[group])

    def cols_of(unit, side, part):
        _layer, start, width, first, _rows = UNITS[unit]
        begin, count = ((0, width), (0, first), (first, width - first))[0 if part is None else part + 1]
        return pl.ds(pl.multiple_of(start + side * width + begin, 128), count)

    def unit_view(unit, rows, side, part=None):
        return w.at[UNITS[unit][0], rows, cols_of(unit, side, part)]

    def rows_of(side):
        return pl.ds(pl.multiple_of(side * (4 * ROWS), 16), 4 * ROWS)

    def block_build(unit):
        layer, start, width, _first, (begin, end) = UNITS[unit]
        block = rows_at(dp * 4 + z)
        for group in range((end - begin) // 16):
            at = begin + 16 * group
            tall = held[layer, :, at : at + 16, :].reshape(256, 128)
            wide = dot(onehot[...], tall).astype(BF)
            for inner in range(4):
                chunk = 4 * group + inner
                if chunk < width // 128:
                    cols = pl.ds(pl.multiple_of(start + core * width + 128 * chunk, 128), 128)
                    w[layer, block, cols] = wide[ROWS * inner : ROWS * inner + ROWS]
        ref = unit_view(unit, block, core)
        turns = range(1, 8 if unit == 0 else 4)
        for turn in turns:
            where = device(turned(dp, turn // 4, 2), turned(z, turn % 4, 4), y, x, core)
            push(ref, ref, gz_send.at[unit], gz_recv.at[unit], where)
        sent(gathers, lambda: w.at[layer, 0 : len(turns) * ROWS, 0:width], gz_send, unit)

    def gather_direct(unit):
        layer, _start, width, _first, _rows = UNITS[unit]
        arrived(unit_view(unit, slice(0, 7 * ROWS), core), gz_send.at[unit], gz_recv.at[unit])
        ref = unit_view(unit, slice(0, D), core)
        push(ref, ref, gs_send.at[unit], gs_recv.at[unit], sibling)
        sent(gathers, lambda: w.at[layer, :, 0:width], gs_send, unit)

    def gather_z(unit):
        layer, _start, width, _first, _rows = UNITS[unit]
        arrived(unit_view(unit, slice(0, 3 * ROWS), core), gz_send.at[unit], gz_recv.at[unit])
        for part in range(2):
            ref = unit_view(unit, rows_of(dp), core, part)
            where = device(1 - dp, z, (y, 1 - y)[part], x, core)
            push(ref, ref, gy_send.at[unit], gy_recv.at[unit], where)
        sent(gathers, lambda: w.at[layer, 0 : 4 * ROWS, 0:width], gy_send, unit)
        ref = unit_view(unit, rows_of(dp), core)
        push(ref, ref, gs_send.at[unit], gs_recv.at[unit], sibling)

    def gather_y(unit):
        layer, _start, width, _first, _rows = UNITS[unit]
        ref = unit_view(unit, rows_of(1 - dp), core)
        arrived(ref, gy_send.at[unit], gy_recv.at[unit])
        push(ref, ref, gs_send.at[unit], gs_recv.at[unit], sibling)
        sent(gathers, lambda: w.at[layer, :, 0:width], gs_send, unit)

    def gather_end(unit):
        arrived(unit_view(unit, slice(0, D), 1 - core), gs_send.at[unit], gs_recv.at[unit])

    moves = ((acts, img), (cot_in, cot))

    def image_copy(index, entry, home):
        source, target = moves[index]
        return copy_to(
            source.at[entry],
            target.at[image_rows(position), :],
            i_send.at[index],
            i_recv.at[index],
            device(dp, z, y, home // 2, home % 2),
        )

    def image_local(index, entry):
        source, target = moves[index]
        return pltpu.make_async_copy(
            source.at[entry], target.at[image_rows(position), :], i_local.at[index]
        )

    def image_send(index):
        for entry, home in enumerate(OWNERS):

            @pl.when(position != home)
            def _():
                image_copy(index, entry, home).start()

            @pl.when(position == home)
            def _():
                image_local(index, entry).start()

    def image_arrive(index):
        source, target = moves[index]

        @pl.when(jnp.logical_not(owner))
        def _():
            target[...] = jnp.zeros_like(target)
            copy_to(source, source, i_send.at[index], i_recv.at[index], sibling).wait_send()

        @pl.when(owner)
        def _():
            image_local(index, 0).wait()
            ref = source.at[0:5]
            copy_to(ref, ref, i_send.at[index], i_recv.at[index], sibling).wait_send()
            arrived(target.at[0 : 7 * 96, :], i_send.at[index], i_recv.at[index])

    def grad_root(unit):
        return active if UNITS[unit][1] == 0 else w

    def grad_view(unit, rows, side, part=None):
        return grad_root(unit).at[UNITS[unit][0], rows, cols_of(unit, side, part)]

    def reduce_core(unit):
        layer, _start, width, _first, _rows = UNITS[unit]
        root = grad_root(unit)
        for index, side in enumerate((1 - dp, dp)):
            push(
                grad_view(unit, rows_of(side), 1 - core),
                core_buf[unit].at[index],
                rc_send.at[unit],
                rc_recv.at[unit, index],
                sibling,
            )
        sent(reduces, lambda: root.at[layer, 0:D, 0:width], rc_send, unit)

    def reduce_y(unit):
        layer, _start, width, first, _rows = UNITS[unit]
        arrived(core_buf[unit].at[0], rc_send.at[unit], rc_recv.at[unit, 0])

        def add(block, carried):
            ref = grad_view(unit, rows_at((1 - dp) * 4 + block), core)
            ref[...] = (ref[...].astype(F32) + core_buf[unit][0, rows_at(block), :].astype(F32)).astype(BF)
            return carried

        lax.fori_loop(0, 4, add, 0)
        for part, cols in enumerate((slice(0, first), slice(first, width))):
            push(
                grad_view(unit, rows_of(1 - dp), core, part),
                y_buf[unit].at[:, cols],
                ry_send.at[unit],
                ry_recv.at[unit],
                device(1 - dp, z, (y, 1 - y)[part], x, core),
            )
        sent(reduces, lambda: y_buf[unit], ry_send, unit)

    def reduce_z(unit):
        layer, _start, width, first, _rows = UNITS[unit]
        arrived(core_buf[unit].at[1], rc_send.at[unit], rc_recv.at[unit, 1])
        arrived(y_buf[unit], ry_send.at[unit], ry_recv.at[unit])
        for turn in (1, 2, 3, 0):
            block = turned(z, turn, 4)
            ref = grad_view(unit, rows_at(dp * 4 + block), core)
            total = (
                ref[...].astype(F32)
                + core_buf[unit][1, rows_at(block), :].astype(F32)
                + y_buf[unit][rows_at(block), :].astype(F32)
            )
            ref[...] = total.astype(BF)
            if turn:
                push(
                    ref,
                    z_buf[unit].at[turn - 1],
                    rz_send.at[unit],
                    rz_recv.at[unit],
                    device(dp, block, y, x, core),
                )
        sent(reduces, lambda: z_buf[unit], rz_send, unit)

    def reduce_direct(unit):
        layer, _start, width, _first, _rows = UNITS[unit]
        for index in range(2):
            arrived(core_buf[unit].at[index], rc_send.at[unit], rc_recv.at[unit, index])
        for turn in (1, 2, 3, 4, 5, 6, 7, 0):
            to_dp, to_z = turned(dp, turn // 4, 2), turned(z, turn % 4, 4)
            ref = grad_view(unit, rows_at(to_dp * 4 + to_z), core)
            total = ref[...].astype(F32) + core_buf[unit][1 - turn // 4, rows_at(to_z), :].astype(F32)
            ref[...] = total.astype(BF)
            if turn:
                push(
                    ref,
                    z_buf[unit].at[turn - 1],
                    rz_send.at[unit],
                    rz_recv.at[unit],
                    device(to_dp, to_z, y, x, core),
                )
        sent(reduces, lambda: z_buf[unit], rz_send, unit)

    def reduce_slab(unit):
        layer, _start, width, _first, (begin, end) = UNITS[unit]
        total = grad_view(unit, rows_at(dp * 4 + z), core)[...].astype(F32)
        arrived(z_buf[unit], rz_send.at[unit], rz_recv.at[unit])
        for turn in range(1, 8 if unit == 0 else 4):
            total = total + z_buf[unit][turn - 1].astype(F32)
        low = total.astype(BF)
        for group in range((end - begin) // 16):
            parts = [
                low[:, 128 * chunk : 128 * chunk + 128]
                if chunk < width // 128
                else jnp.zeros((ROWS, 128), BF)
                for chunk in range(4 * group, 4 * group + 4)
            ]
            tall = dot_tn(onehot[...], jnp.concatenate(parts, axis=0)).astype(BF)
            at = begin + 16 * group
            slabs[layer, :, at : at + 16, :] = tall.reshape(SPLIT, 16, 128)

    def reduce_plane(group):
        layer, begin, end = GROUPS[group]
        for turn in range(1, 16):
            to_y, to_x, to_core = plane_target(turn)
            push(
                slabs.at[layer, to_y * 8 + to_x * 2 + to_core, begin:end, :],
                ends.at[layer, turn, begin:end, :],
                rp_send.at[group],
                rp_recv.at[group],
                device(dp, z, to_y, to_x, to_core),
            )
        sent(reduces, lambda: slabs.at[layer, 1:16, begin:end, :], rp_send, group)

    outs = ((o_qkv, 0, 9), (o_out, 10, 13), (o_up, 13, 25), (o_down, 25, 37))

    def reduce_end(group):
        layer, begin, end = GROUPS[group]
        totals = [slabs[layer, mine, begin:end, :].astype(F32), None]
        arrived(ends.at[layer, 1:16, begin:end, :], rp_send.at[group], rp_recv.at[group])
        for turn in range(1, 16):
            value = ends[layer, turn, begin:end, :].astype(F32)
            side = turn % 2
            totals[side] = value if totals[side] is None else totals[side] + value
        first = core == 0
        halves = (
            jnp.where(first, totals[0], totals[1]),
            jnp.where(first, totals[1], totals[0]),
        )
        for of, start, width, _first, (low, high) in UNITS:
            for chunk in range(width // 64) if of == layer and begin <= low and high <= end else ():
                inner = low - begin + 4 * (chunk % (width // 128))
                rows = halves[chunk // (width // 128)][inner : inner + 3]
                for target, lowest, highest in outs:
                    if lowest <= start // 128 + chunk < highest:
                        at = 128 * (start // 128 + chunk - lowest)
                        target[:, layer, at : at + 128] = rows

    def misc_out(layer, total):
        tall_sums[...] = jnp.concatenate([total, jnp.zeros((120, D), F32)], axis=0).T
        at = lax.broadcasted_iota(jnp.int32, (8, 128), 0)
        rows = jnp.zeros((8, 128), F32)
        for feature in range(3):
            line = tall_sums[pl.ds(3 * (dp * 64 + sp) + feature, 1), :]
            o_biases[feature, layer : layer + 1, :] = line[:, 2:8]
            rows = jnp.where(at == feature, line, rows)
        wide = jnp.concatenate([rows, jnp.zeros((120, 128), F32)], axis=0).T
        o_gains[layer] = wide[0:2, 0:3]

    def early_sum(stage):
        def send(source, target, where):
            push(source, target, h_send.at[stage], h_recv.at[stage], where)

        def wait(ref):
            arrived(ref, h_send.at[stage - 1], h_recv.at[stage - 1])

        if stage == 0:
            for layer in range(LAYERS):
                early[3 * layer : 3 * layer + 3, :] = hid_sums[layer]
            early[8:16, 0:D] = row_sums[1]
            send(early, h_core, sibling)
            sent(reduces, lambda: early, h_send, 0)
        elif stage == 1:
            wait(h_core)
            h_sum[0] = early[...] + h_core[...]
            send(h_sum.at[0], h_y, device(1 - dp, z, y, x, core))
            sent(reduces, lambda: early, h_send, 1)
        elif stage == 2:
            wait(h_y)
            h_sum[1] = h_sum[0] + h_y[...]
            for turn in range(1, 4):
                send(h_sum.at[1], h_z.at[turn - 1], device(dp, turned(z, turn, 4), y, x, core))
            sent(reduces, lambda: h_z, h_send, 2)
        elif stage == 3:
            wait(h_z)
            h_sum[2] = h_sum[1] + h_z[0] + h_z[1] + h_z[2]
            for turn in range(1, 8):
                where = device(dp, z, turned(y, turn // 4, 2), turned(x, turn % 4, 4), core)
                send(h_sum.at[2], h_p.at[turn], where)
            sent(reduces, lambda: h_p.at[1:8], h_send, 3)
        else:
            wait(h_p.at[1:8])
            total = h_sum[2]
            for turn in range(1, 8):
                total = total + h_p[turn]
            for layer in range(LAYERS):
                for chunk in range(FF // FC):
                    hid[layer, :, FC * chunk : FC * chunk + FC] = total[
                        3 * layer + chunk : 3 * layer + chunk + 1
                    ]
            for layer in range(LAYERS):
                share = pl.ds(pl.multiple_of(dp * (FF // 2), 128), FF // 2)
                o_hid[layer : layer + 1, :] = hid[layer, :, share]
            misc_out(1, total[8:16, 0:D])

    def late_sum(stage):
        if stage == 0:
            late[...] = row_sums[0]
            for turn in range(1, 16):
                where = device(dp, z, *plane_target(turn))
                push(late, l_plane.at[turn], l_send.at[0], l_recv.at[0], where)
            sent(reduces, lambda: l_plane.at[1:16], l_send, 0)
        elif stage == 1:
            arrived(l_plane.at[1:16], l_send.at[0], l_recv.at[0])
            total = late[...]
            for turn in range(1, 16):
                total = total + l_plane[turn]
            l_sum[...] = total
            for turn in range(1, 8):
                where = device(turned(dp, turn // 4, 2), turned(z, turn % 4, 4), y, x, core)
                push(l_sum, l_far.at[turn], l_send.at[1], l_recv.at[1], where)
            sent(reduces, lambda: l_far.at[1:8], l_send, 1)
        else:
            arrived(l_far.at[1:8], l_send.at[1], l_recv.at[1])
            total = l_sum[...]
            for turn in range(1, 8):
                total = total + l_far[turn]
            misc_out(0, total)

    backs = ((act, act_out), (igrad, igrad_out))

    def back_copy(index, home):
        source, target = backs[index]
        return copy_to(
            source.at[96 * home : 96 * home + 96, :],
            target.at[entry_mine],
            e_send.at[index],
            e_recv.at[index],
            device(dp, z, y, home // 2, home % 2),
        )

    def back_local(index, home):
        source, target = backs[index]
        return pltpu.make_async_copy(
            source.at[96 * home : 96 * home + 96, :], target.at[entry_mine], e_local.at[index]
        )

    def back_send(index, first, last):
        for home in range(first, last):

            @pl.when(jnp.logical_and(owner, position != home))
            def _():
                back_copy(index, home).start()

            @pl.when(jnp.logical_and(owner, position == home))
            def _():
                back_local(index, home).start()

    def back_arrive(index):
        source, target = backs[index]

        @pl.when(owner)
        def _():
            back_local(index, 0).wait()
            ref = source.at[0 : 7 * 96, :]
            copy_to(ref, ref, e_send.at[index], e_recv.at[index], sibling).wait_send()
            arrived(target.at[0:5], e_send.at[index], e_recv.at[index])

        @pl.when(jnp.logical_not(owner))
        def _():
            arrived(target, e_send.at[index], e_recv.at[index])

    length = lengths[jnp.minimum(entry_mine, 5), lax.div(dp * 64 + sp, 8)]
    (
        project, attend, feed, turn_back, unfeed, feed_grads, unproject_out, unattend, qkv_grads, unproject,
    ) = encoder(
        length, w, carry, inputs, cot, act, igrad, hid, hid_sums, row_sums,
        mids, qkv, probs_even, probs_odd, invs, att, att_low, active, slope, low_a, low_b, dqkv, trans, trans_b, prm,
    )

    def run(layer, *steps):
        for of in range(LAYERS):
            chosen = [step for step in steps if step[0] == of]
            if chosen:

                @pl.when(layer == of)
                def _():
                    for _of, function, *arguments in chosen:
                        function(*arguments)

    def pairs(body, layer, hooks):
        def one(pair, carried):
            body(layer, pair)
            for at, of, function, *arguments in hooks:

                @pl.when(jnp.logical_and(pair == at, layer == of))
                def _():
                    function(*arguments)

            return carried

        lax.fori_loop(0, PAIRS, one, 0)

    def hidden_arrive():
        arrived(hid_all.at[1 - dp], b_send.at[0], b_recv.at[0])
        for side in range(2):
            for layer in range(LAYERS):
                hid[layer, :, side * (FF // 2) : (side + 1) * (FF // 2)] = hid_all[side, layer : layer + 1, :]

    slab_send(0)
    image_send(0)
    slab_send(1)
    slab_build_layer(1)
    hid_all[dp] = p_hid[...].astype(F32)
    push(hid_all.at[dp], hid_all.at[dp], b_send.at[0], b_recv.at[0], device(1 - dp, z, y, x, core))
    sent(gathers, lambda: hid_all.at[0], b_send, 0)
    onehot[...] = spread_matrix()
    invs[...] = jnp.zeros_like(invs)
    hid_sums[...] = jnp.zeros_like(hid_sums)
    row_sums[...] = jnp.zeros_like(row_sums)
    early[...] = jnp.zeros_like(early)
    slab_arrive(0)
    block_build(0)
    slab_send(2)
    slab_arrive(1)
    block_build(1)
    block_build(2)
    gather_direct(0)
    gather_z(1)
    slab_arrive(2)
    block_build(3)
    block_build(4)
    image_arrive(0)
    carry[...] = img[...].astype(F32)
    gather_z(2)
    gather_end(0)

    def forward(layer, carried):
        project(layer)
        run(layer, (0, gather_y, 1))
        pairs(
            attend,
            layer,
            ((0, 0, gather_z, 3), (0, 0, image_send, 1), (1, 0, gather_y, 2), (1, 1, gather_y, 4)),
        )
        run(
            layer,
            (0, gather_z, 4),
            (0, gather_y, 3),
            (0, hidden_arrive),
            (0, gather_end, 1),
            (0, gather_end, 2),
            (1, gather_end, 4),
        )
        feed(layer)
        run(layer, (0, gather_end, 3))
        return carried

    lax.fori_loop(0, LAYERS, forward, 0)
    back_send(0, 0, 8)
    image_arrive(1)
    turn_back()
    all_sent(gathers)

    def backward(step, carried):
        layer = LAYERS - 1 - step
        unfeed(layer)
        run(layer, (0, early_sum, 0), (0, reduce_z, 4), (0, reduce_y, 3))
        feed_grads(layer)
        run(layer, (0, reduce_core, 2))
        unproject_out(layer)
        run(
            layer,
            (1, reduce_core, 4),
            (0, reduce_core, 1),
            (0, early_sum, 1),
            (0, reduce_z, 3),
            (0, reduce_y, 2),
        )
        pairs(
            unattend,
            layer,
            (
                (0, 0, reduce_y, 1),
                (1, 0, early_sum, 2),
                (1, 0, reduce_slab, 4),
                (1, 0, reduce_z, 2),
                (1, 1, reduce_y, 4),
                (2, 0, reduce_z, 1),
            ),
        )
        run(layer, (0, reduce_slab, 3), (0, reduce_plane, 2), (0, early_sum, 3))
        qkv_grads(layer)
        run(layer, (1, reduce_core, 3), (0, reduce_core, 0))
        unproject(layer, lambda: run(layer, (0, back_send, 1, 0, 4), (0, reduce_direct, 0)))
        return carried

    lax.fori_loop(0, LAYERS, backward, 0)
    late_sum(0)
    back_send(1, 4, 8)
    early_sum(4)
    late_sum(1)
    reduce_end(2)
    reduce_slab(2)
    reduce_slab(1)
    reduce_plane(1)
    reduce_slab(0)
    reduce_plane(0)
    late_sum(2)
    reduce_end(1)
    for index in range(2):
        back_arrive(index)
    reduce_end(0)
    all_sent(reduces)


def finish_kernel(
    i_qkv, i_out, i_up, i_down, i_gains, i_biases, i_hid, i_act, i_igrad,
    act, igrad, g_qkv, g_out, g_up, g_down, g_gains, g_biases, g_hid,
):
    act[...] = i_act[...].astype(F32)
    igrad[...] = i_igrad[...].astype(F32)
    for source, target in (
        (i_qkv, g_qkv),
        (i_out, g_out),
        (i_up, g_up),
        (i_down, g_down),
        (i_gains, g_gains),
        (i_biases, g_biases),
        (i_hid, g_hid),
    ):
        target[...] = source[...]


def local(acts, cotangent, lengths, w_qkv, w_out, w_up, w_down, gains, biases, hidden_bias):
    swap = lambda array: array.transpose(1, 0, 2)
    vmem = pl.BlockSpec(memory_space=pltpu.VMEM)
    any_space = pl.BlockSpec(memory_space=pl.ANY)
    shape = jax.ShapeDtypeStruct
    buffer = pltpu.VMEM
    dma = pltpu.SemaphoreType.DMA
    pair = lambda *dims: [dma(dims), dma(dims)]
    results = pl.pallas_call(
        kernel,
        out_shape=(
            shape((3, LAYERS, 3 * D), F32),
            shape((3, LAYERS, D), F32),
            shape((3, LAYERS, FF), F32),
            shape((3, LAYERS, FF), F32),
            shape((LAYERS, 2, 3), F32),
            shape((3, LAYERS, 6), F32),
            shape((LAYERS, FF // 2), F32),
            shape((6, 96, D), BF),
            shape((6, 96, D), BF),
        ),
        in_specs=[pl.BlockSpec(memory_space=pltpu.SMEM), any_space, any_space] + [vmem] * 7,
        out_specs=(vmem,) * 7 + (any_space,) * 2,
        scratch_shapes=[
            buffer((LAYERS, D, WIDE), BF),
            buffer((TOK, D), F32),
            buffer((LAYERS, TOK, D), F32),
            buffer((TOK, D), BF),
            buffer((TOK, D), BF),
            buffer((TOK, D), BF),
            buffer((4 * ROWS, 256), BF),
            buffer((SLAB, 128), F32),
            buffer((2, LAYERS, FF // 2), F32),
            buffer((LAYERS, 1, FF), F32),
            buffer((LAYERS, 3, FC), F32),
            buffer((LAYERS, 8, D), F32),
            buffer((16, FC), F32),
            buffer((8, D), F32),
            buffer((D, 128), F32),
            *compute_scratch(),
            buffer((LAYERS, 2, SLAB, 128), BF),
            buffer((LAYERS, SPLIT, SLAB, 128), BF),
            buffer((LAYERS, SPLIT, SLAB, 128), BF),
            buffer((LAYERS, SPLIT, SLAB, 128), BF),
            buffer((16, FC), F32),
            buffer((16, FC), F32),
            buffer((3, 16, FC), F32),
            buffer((8, 16, FC), F32),
            buffer((3, 16, FC), F32),
            buffer((16, 8, D), F32),
            buffer((8, 8, D), F32),
            buffer((8, D), F32),
        ]
        + pair(len(GROUPS))
        + pair(COUNT)
        + pair(COUNT)
        + pair(COUNT)
        + [dma((2,)), dma((2,)), dma((2,)), dma((1,)), dma((1,))]
        + [dma((COUNT,)), dma((COUNT, 2))]
        + pair(COUNT)
        + pair(COUNT)
        + pair(len(GROUPS))
        + [dma((2,)), dma((2,)), dma((2,))]
        + pair(4)
        + pair(2)
        + [buffer((2, 4 * ROWS, unit[2]), BF) for unit in UNITS]
        + [buffer((4 * ROWS if index else 16, unit[2]), BF) for index, unit in enumerate(UNITS)]
        + [buffer((3 if index else 7, ROWS, unit[2]), BF) for index, unit in enumerate(UNITS)],
        compiler_params=pltpu.CompilerParams(
            collective_id=0, has_side_effects=True, vmem_limit_bytes=63 * MIB
        ),
        name="encoder",
    )(
        lengths, acts, cotangent, swap(w_qkv), swap(w_out), swap(w_up), swap(w_down),
        gains.transpose(0, 2, 1), swap(biases), hidden_bias,
    )
    act, igrad, g_qkv, g_out, g_up, g_down, g_gains, g_biases, g_hid = pl.pallas_call(
        finish_kernel,
        out_shape=(
            shape((6, 96, D), F32),
            shape((6, 96, D), F32),
            shape((3, LAYERS, 3 * D), F32),
            shape((3, LAYERS, D), F32),
            shape((3, LAYERS, FF), F32),
            shape((3, LAYERS, FF), F32),
            shape((LAYERS, 2, 3), F32),
            shape((3, LAYERS, 6), F32),
            shape((LAYERS, FF // 2), F32),
        ),
        in_specs=[vmem] * 9,
        out_specs=(vmem,) * 9,
        name="finish",
    )(*results)
    return (
        act,
        igrad,
        swap(g_qkv),
        swap(g_out),
        swap(g_up),
        swap(g_down),
        g_gains.transpose(0, 2, 1),
        swap(g_biases),
        g_hid,
    )


def solution(mesh):
    split = P(None, ("dp", "sp"), None)
    return jax.shard_map(
        local,
        mesh=mesh,
        in_specs=(split, split, P(), split, split, split, split, split, split, P(None, "dp")),
        out_specs=(split,) * 8 + (P(None, "dp"),),
        check_vma=False,
    )
```

```python
import math

import jax
import jax.numpy as jnp
from jax import lax
from jax.experimental import pallas as pl
from jax.experimental.pallas import tpu as pltpu
from jax.sharding import PartitionSpec as P

D = 384
HEADS = 6
PAIRS = HEADS // 2
HEAD_DIM = 64
FF = 1536
LAYERS = 2
TOK = 768
EPSILON = 1e-06
NEG_FILL = -1e30
GELU_COEF = math.sqrt(2.0 / math.pi)
CUBIC_COEF = 0.044715
BF = jnp.bfloat16
F32 = jnp.float32
RB = 384
FC = 512
MIB = 1024 * 1024

MISC0, OUT0, UP0, DOWN0, WIDE = 1152, 1280, 1664, 3200, 4864
UNITS = (
    (0, 0, 640, 384, (0, 32)),
    (0, 1280, 896, 384, (32, 64)),
    (0, 3072, 896, 384, (64, 96)),
    (1, 0, 640, 384, (0, 32)),
    (1, 1280, 1792, 896, (32, 96)),
)
COUNT = len(UNITS)
SLAB = 96
GROUPS = ((0, 0, 32), (0, 32, 96), (1, 0, 96))

OWNERS = (0, 1, 2, 4, 5, 6)
MESH = pl.DeviceIdType.MESH
SPLIT = 16
ROWS = 48


def dot(left_side, right_side):
    return jnp.dot(left_side, right_side, preferred_element_type=F32)


def dot_nt(left_side, right_side):
    return lax.dot_general(
        left_side, right_side, (((1,), (1,)), ((), ())), preferred_element_type=F32
    )


def dot_tn(left_side, right_side):
    return lax.dot_general(
        left_side, right_side, (((0,), (0,)), ((), ())), preferred_element_type=F32
    )


def normalized(values):
    center = values - jnp.mean(values, axis=-1, keepdims=True)
    inverse = lax.rsqrt(jnp.mean(center * center, axis=-1, keepdims=True) + EPSILON)
    return center * inverse, inverse


def norm_backward(upstream, xhat, inverse, gain):
    scaled = upstream * gain
    return inverse * (
        scaled
        - jnp.mean(scaled, axis=-1, keepdims=True)
        - xhat * jnp.mean(scaled * xhat, axis=-1, keepdims=True)
    )


def gelu_pair(hidden):
    square = hidden * hidden
    tangent = jnp.tanh(hidden * (GELU_COEF + (GELU_COEF * CUBIC_COEF) * square))
    half = 0.5 + 0.5 * tangent
    active = hidden * half
    slope = half + active * (1.0 - tangent) * (
        GELU_COEF + (3.0 * GELU_COEF * CUBIC_COEF) * square
    )
    return active, slope


def colsum(values):
    return jnp.sum(values.astype(F32), axis=0, keepdims=True)


def each_block(body, count=RB):
    for start in range(0, TOK, count):
        body(slice(start, start + count))


def each_chunk(stop, width, body):
    for start in range(0, stop, width):
        body(slice(start, start + width), lambda base, at=start: slice(base + at, base + at + width))


def encoder(
    length, w, carry, inputs, cot, act, igrad, hid, hid_sums, row_sums,
    mids, qkv, probs_even, probs_odd, invs, att, att_low, active, slope, low_a, low_b, dqkv, trans, trans_b, prm,
):
    last_valid = lax.broadcasted_iota(jnp.int32, (1, 128), 1) + (TOK - 128) < length
    lanes = lax.broadcasted_iota(jnp.int32, (1, 128), 1)
    first_half = lanes < 64
    scale = HEAD_DIM ** (-0.5)

    def lanes_at(pair, base):
        return pl.ds(pl.multiple_of(base + 128 * pair, 128), 128)

    def half_of(block, which):
        keep = first_half if which == 0 else jnp.logical_not(first_half)
        return jnp.where(keep, block, jnp.zeros_like(block))

    def row(layer, index):
        at = (index + 6) % 8
        return prm[layer, at : at + 1, :]

    def project(layer):
        prm[layer] = w[layer, :, MISC0 : MISC0 + 128].astype(F32).T[0:8]

        bias = jnp.concatenate([row(layer, 2), jnp.zeros((1, D), F32), row(layer, 3)], axis=1)

        def body(rows):
            source = carry[rows, :]
            inputs[layer, rows, :] = source
            xhat, _inverse = normalized(source)
            low = (xhat * row(layer, 0) + row(layer, 5)).astype(BF)
            qkv[layer, rows, :] = (dot(low, w[layer, :, 0 : 3 * D]) + bias).astype(BF)

        each_block(body)
        trans[...] = qkv[layer, :, D : 2 * D].T

    def attend(layer, pair):
        lane = lanes_at(pair, 0)
        value = qkv[layer, :, lanes_at(pair, 2 * D)]
        value = jnp.concatenate([value, jnp.ones((TOK, 128), BF)], axis=1)

        def body(rows):
            query = qkv[layer, rows, lane] * jnp.asarray(scale, BF)
            results = []
            kept = invs[rows, :]
            for which in range(2):
                head = 2 * pair + which
                scores = dot(half_of(query, which), trans[lane, :])
                last = jnp.where(last_valid, scores[:, TOK - 128 :], NEG_FILL)
                scores = jnp.concatenate([scores[:, : TOK - 128], last], axis=1)
                low = jnp.exp(scores - jnp.max(scores, axis=-1, keepdims=True)).astype(BF)
                (probs_even, probs_odd)[which][layer, pair, rows, :] = low
                product = dot(low, value)
                inverse = 1.0 / product[:, 128:]
                results.append(product[:, :128] * inverse)
                kept = jnp.where(lanes == 8 * layer + head, inverse, kept)
            invs[rows, :] = kept
            whole = jnp.where(first_half, results[0], results[1])
            high = whole.astype(BF)
            att[layer, rows, lane] = high
            att_low[layer, rows, lane] = (whole - high.astype(F32)).astype(BF)

        each_block(body)

    def feed(layer):
        def body(rows):
            mid = inputs[layer, rows, :] + (
                dot(att[layer, rows, :], w[layer, :, OUT0 : OUT0 + D]) + row(layer, 4)
            )
            mids[layer, rows, :] = mid
            xhat, _inverse = normalized(mid)
            low = (xhat * row(layer, 1) + row(layer, 6)).astype(BF)
            total = mid + row(layer, 7)
            for chunk in range(FF // FC):
                cols = slice(FC * chunk, FC * chunk + FC)
                hidden = dot(low, w[layer, :, UP0 + FC * chunk : UP0 + FC * chunk + FC])
                value, rate = gelu_pair(hidden + hid[layer, :, cols])
                value = value.astype(BF)
                active[layer, rows, cols] = value
                slope[layer, rows, cols] = rate.astype(BF)
                total = total + dot_nt(
                    value, w[layer, :, DOWN0 + FC * chunk : DOWN0 + FC * chunk + FC]
                )
            carry[rows, :] = total
            act[rows, :] = total.astype(BF)

        each_block(body)

    def add_sum(layer, index, values):
        row_sums[layer, index : index + 1, :] += colsum(values)

    def turn_back():
        carry[...] = cot[...].astype(F32)

    def unfeed(layer):
        def body(rows):
            upstream = carry[rows, :]
            down = upstream.astype(BF)
            low_a[rows, :] = down
            add_sum(layer, 7, down)
            xhat, inverse = normalized(mids[layer, rows, :])
            low_b[rows, :] = (xhat * row(layer, 1) + row(layer, 6)).astype(BF)
            total = jnp.zeros((RB, D), F32)
            for chunk in range(FF // FC):
                cols = slice(FC * chunk, FC * chunk + FC)
                grad = dot(down, w[layer, :, DOWN0 + FC * chunk : DOWN0 + FC * chunk + FC])
                grad = (grad * slope[layer, rows, cols].astype(F32)).astype(BF)
                slope[layer, rows, cols] = grad
                hid_sums[layer, chunk : chunk + 1, :] += colsum(grad)
                total = total + dot_nt(grad, w[layer, :, UP0 + FC * chunk : UP0 + FC * chunk + FC])
            add_sum(layer, 1, total * xhat)
            add_sum(layer, 6, total)
            carry[rows, :] = upstream + norm_backward(total, xhat, inverse, row(layer, 1))

        each_block(body)

    def feed_grads(layer):
        trans[...] = low_a[...].T
        trans_b[...] = low_b[...].T

        def grad_down(cols, at):
            w[layer, :, at(DOWN0)] = dot(trans[...], active[layer, :, cols]).astype(BF)

        def grad_up(cols, at):
            w[layer, :, at(UP0)] = dot(trans_b[...], slope[layer, :, cols]).astype(BF)

        each_chunk(FF, FC, grad_down)
        each_chunk(FF, FC, grad_up)

    def unproject_out(layer):
        def body(rows):
            low = carry[rows, :].astype(BF)
            low_a[rows, :] = low
            add_sum(layer, 4, low)
            grad = dot_nt(low, w[layer, :, OUT0 : OUT0 + D])
            inverse = jnp.where(layer == 0, invs[rows, 0:8], invs[rows, 8:16])
            for pair in range(PAIRS):
                lane = slice(128 * pair, 128 * pair + 128)
                both = jnp.where(
                    first_half,
                    inverse[:, 2 * pair : 2 * pair + 1],
                    inverse[:, 2 * pair + 1 : 2 * pair + 2],
                )
                low_b[rows, lane] = (grad[:, lane] * both).astype(BF)

        each_block(body)
        trans[...] = att[layer].T
        w[layer, :, OUT0 : OUT0 + D] = dot(trans[...], low_a[...]).astype(BF)
        trans[...] = low_b[...].T
        trans_b[...] = (qkv[layer, :, 0:D] * jnp.asarray(scale, BF)).T

    def unattend(layer, pair):
        lane = lanes_at(pair, 0)
        key = qkv[layer, :, lanes_at(pair, D)]
        value = qkv[layer, :, lanes_at(pair, 2 * D)]
        key_parts, value_parts = [0.0, 0.0], [0.0, 0.0]

        def body(rows):
            grad = low_b[rows, lane]
            whole = att[layer, rows, lane].astype(F32) + att_low[layer, rows, lane].astype(F32)
            weighted = grad.astype(F32) * whole
            results = []
            for which, probs in enumerate((probs_even, probs_odd)):
                feature = pl.ds(pl.multiple_of(128 * pair + 64 * which, 64), 64)
                low = probs[layer, pair, rows, :]
                inner = jnp.sum(half_of(weighted, which), axis=-1, keepdims=True)
                prob_grad = dot_nt(half_of(grad, which), value)
                score_grad = (low.astype(F32) * (prob_grad - inner)).astype(BF)
                results.append(dot(score_grad, key))
                key_parts[which] += dot(trans_b[feature, rows], score_grad)
                value_parts[which] += dot(trans[feature, rows], low)
            dqkv[rows, lane] = (jnp.where(first_half, results[0], results[1]) * scale).astype(BF)

        each_block(body, 768)
        dqkv[:, lanes_at(pair, D)] = jnp.concatenate(key_parts, axis=0).T.astype(BF)
        dqkv[:, lanes_at(pair, 2 * D)] = jnp.concatenate(value_parts, axis=0).T.astype(BF)

    def qkv_grads(layer):
        def body(rows):
            xhat, _inverse = normalized(inputs[layer, rows, :])
            low_a[rows, :] = (xhat * row(layer, 0) + row(layer, 5)).astype(BF)

        each_block(body)
        trans[...] = low_a[...].T

        def grad_qkv(cols, _at):
            active[layer, 0:D, cols] = dot(trans[...], dqkv[:, cols]).astype(BF)

        each_chunk(3 * D, D, grad_qkv)

    def unproject(layer, between):
        def body(rows):
            if rows.stop == TOK:
                between()
            add_sum(layer, 2, dqkv[rows, 0:D])
            add_sum(layer, 3, dqkv[rows, 2 * D : 3 * D])
            xhat, inverse = normalized(inputs[layer, rows, :])
            total = dot_nt(dqkv[rows, :], w[layer, :, 0 : 3 * D])
            add_sum(layer, 0, total * xhat)
            add_sum(layer, 5, total)
            upstream = carry[rows, :] + norm_backward(total, xhat, inverse, row(layer, 0))
            carry[rows, :] = upstream
            igrad[rows, :] = upstream.astype(BF)

        each_block(body)

    return (
        project, attend, feed, turn_back, unfeed, feed_grads, unproject_out, unattend, qkv_grads, unproject,
    )


def compute_scratch():
    return [
        pltpu.VMEM((LAYERS, TOK, D), F32),
        pltpu.VMEM((LAYERS, TOK, 3 * D), BF),
        pltpu.VMEM((LAYERS, PAIRS, TOK, TOK), BF),
        pltpu.VMEM((LAYERS, PAIRS, TOK, TOK), BF),
        pltpu.VMEM((TOK, 128), F32),
        pltpu.VMEM((LAYERS, TOK, D), BF),
        pltpu.VMEM((LAYERS, TOK, D), BF),
        pltpu.VMEM((LAYERS, TOK, FF), BF),
        pltpu.VMEM((LAYERS, TOK, FF), BF),
        pltpu.VMEM((TOK, D), BF),
        pltpu.VMEM((TOK, 3 * D), BF),
        pltpu.VMEM((D, TOK), BF),
        pltpu.VMEM((D, TOK), BF),
        pltpu.VMEM((LAYERS, 8, D), F32),
    ]


def device(dp, z, y, x, core):
    return (dp, z * 16 + y * 8 + x * 2 + core)


def turned(value, by, count):
    return lax.rem(value + (by + count), count)


def rows_at(block):
    return pl.ds(pl.multiple_of(block * ROWS, 16), ROWS)


def image_rows(position):
    return pl.ds(pl.multiple_of(position * 96, 16), 96)


def copy_to(source, target, send, recv, where):
    return pltpu.make_async_remote_copy(
        src_ref=source,
        dst_ref=target,
        send_sem=send,
        recv_sem=recv,
        device_id=where,
        device_id_type=MESH,
    )


def spread_matrix():
    out = lax.broadcasted_iota(jnp.int32, (4 * ROWS, 256), 0)
    col = lax.broadcasted_iota(jnp.int32, (4 * ROWS, 256), 1)
    member, inner, row = col >> 4, (col >> 2) & 3, col & 3
    hit = jnp.logical_and(out == ROWS * inner + 3 * member + row, row < 3)
    return jnp.where(hit, 1.0, 0.0).astype(BF)


def kernel(
    lengths, acts, cot_in, p_qkv, p_out, p_up, p_down, p_gains, p_biases, p_hid,
    o_qkv, o_out, o_up, o_down, o_gains, o_biases, o_hid, act_out, igrad_out,
    w, carry, inputs, img, cot, act, onehot, slab_build, hid_all, hid, hid_sums, row_sums, early, late, tall_sums,
    mids, qkv, probs_even, probs_odd, invs, att, att_low, active, slope, low_b, dqkv, trans, trans_b, prm,
    give, held, slabs, ends,
    h_core, h_y, h_z, h_p, h_sum, l_plane, l_far, l_sum,
    ga_send, ga_recv, gz_send, gz_recv, gy_send, gy_recv, gs_send, gs_recv,
    i_send, i_recv, i_local, b_send, b_recv,
    rc_send, rc_recv, ry_send, ry_recv, rz_send, rz_recv, rp_send, rp_recv,
    e_send, e_recv, e_local, h_send, h_recv, l_send, l_recv,
    *buffers,
):
    core_buf, y_buf, z_buf = [buffers[COUNT * kind : COUNT * kind + COUNT] for kind in range(3)]
    dp, sp = lax.axis_index("dp"), lax.axis_index("sp")
    z = lax.div(sp, 16)
    y = lax.rem(lax.div(sp, 8), 2)
    x = lax.rem(lax.div(sp, 2), 4)
    core = lax.rem(sp, 2)
    mine = y * 8 + x * 2 + core
    position = x * 2 + core
    entry_mine = position - lax.div(position, 4)
    owner = lax.rem(position, 4) < 3
    sibling = device(dp, z, y, x, 1 - core)
    igrad = img
    low_a = cot
    gathers, reduces = [], []

    def push(source, target, send, recv, where):
        copy_to(source, target, send, recv, where).start()

    def all_sent(steps):
        for view, sem, index in steps:
            ref, sem = view(), sem.at[index]
            copy_to(ref, ref, sem, sem, sibling).wait_send()

    def sent(steps, view, sem, *index):
        steps.append((view, sem, index))

    def arrived(ref, send, recv):
        copy_to(ref, ref, send, recv, sibling).wait_recv()

    peers = [sibling]
    for step in range(1, 4):
        peers.append(device(dp, z, y, turned(x, step, 4), core))
        peers.append(device(dp, z, y, turned(x, step, 4), 1 - core))
        peers.append(device(dp, turned(z, step, 4), y, x, core))
        peers.append(device(1 - dp, turned(z, step, 4), y, x, core))
    for step in range(4):
        peers.append(device(dp, z, 1 - y, turned(x, step, 4), core))
        peers.append(device(dp, z, 1 - y, turned(x, step, 4), 1 - core))
    for side in (y, 1 - y):
        peers.append(device(1 - dp, z, side, x, core))
    barrier = pltpu.get_barrier_semaphore()
    for peer in peers:
        pl.semaphore_signal(barrier, inc=1, device_id=peer, device_id_type=MESH)

    def misc_rows(layer):
        slab_build[0:8, :] = jnp.zeros((8, 128), F32)
        slab_build[0:3, 0:6] = p_biases[...].astype(F32)[:, layer, :]
        rows = slab_build[0:3, :]
        at = lax.broadcasted_iota(jnp.int32, (3, 128), 0)
        lane = lax.broadcasted_iota(jnp.int32, (3, 128), 1)
        gains = p_gains[...].astype(F32)
        for gain in range(2):
            for feature in range(3):
                hit = jnp.logical_and(at == feature, lane == 6 + gain)
                rows = jnp.where(hit, gains[layer, gain : gain + 1, feature : feature + 1], rows)
        return rows

    def slab_build_layer(layer):
        whole = jnp.concatenate(
            [p_qkv[...].astype(F32)[:, layer, :], misc_rows(layer)]
            + [ref[...].astype(F32)[:, layer, :] for ref in (p_out, p_up, p_down)]
            + [jnp.zeros((3, 128), F32)],
            axis=1,
        )
        for side in range(2):
            slab_build[...] = jnp.zeros_like(slab_build)
            for of, start, width, _first, rows in UNITS:
                for chunk in range(width // 128) if of == layer else ():
                    at = start + side * width + 128 * chunk
                    row = rows[0] + 4 * chunk
                    slab_build[row : row + 3, :] = whole[:, at : at + 128]
            give[layer, side] = slab_build[...].astype(BF)

    slab_build_layer(0)
    pl.semaphore_wait(barrier, len(peers))

    def plane_target(turn):
        return turned(y, turn // 8, 2), turned(x, turn // 2 % 4, 4), turned(core, turn % 2, 2)

    def plane_source(turn):
        return (
            turned(y, -(turn // 8), 2) * 8
            + turned(x, -(turn // 2 % 4), 4) * 2
            + turned(core, -(turn % 2), 2)
        )

    def slab_send(group):
        layer, begin, end = GROUPS[group]
        held[layer, mine, begin:end, :] = give[layer, core, begin:end, :]
        for turn in range(1, 16):
            to_y, to_x, to_core = plane_target(turn)
            push(
                give.at[layer, to_core, begin:end, :],
                held.at[layer, mine, begin:end, :],
                ga_send.at[group],
                ga_recv.at[group],
                device(dp, z, to_y, to_x, to_core),
            )
        sent(gathers, lambda: held.at[layer, 1:16, begin:end, :], ga_send, group)

    def slab_arrive(group):
        layer, begin, end = GROUPS[group]
        arrived(held.at[layer, 1:16, begin:end, :], ga_send.at[group], ga_recv.at[group])

    def cols_of(unit, side, part):
        _layer, start, width, first, _rows = UNITS[unit]
        begin, count = ((0, width), (0, first), (first, width - first))[0 if part is None else part + 1]
        return pl.ds(pl.multiple_of(start + side * width + begin, 128), count)

    def unit_view(unit, rows, side, part=None):
        return w.at[UNITS[unit][0], rows, cols_of(unit, side, part)]

    def rows_of(side):
        return pl.ds(pl.multiple_of(side * (4 * ROWS), 16), 4 * ROWS)

    def block_build(unit):
        layer, start, width, _first, (begin, end) = UNITS[unit]
        block = rows_at(dp * 4 + z)
        for group in range((end - begin) // 16):
            at = begin + 16 * group
            tall = held[layer, :, at : at + 16, :].reshape(256, 128)
            wide = dot(onehot[...], tall).astype(BF)
            for inner in range(4):
                chunk = 4 * group + inner
                if chunk < width // 128:
                    cols = pl.ds(pl.multiple_of(start + core * width + 128 * chunk, 128), 128)
                    w[layer, block, cols] = wide[ROWS * inner : ROWS * inner + ROWS]
        ref = unit_view(unit, block, core)
        turns = range(1, 8 if unit == 0 else 4)
        for turn in turns:
            where = device(turned(dp, turn // 4, 2), turned(z, turn % 4, 4), y, x, core)
            push(ref, ref, gz_send.at[unit], gz_recv.at[unit], where)
        sent(gathers, lambda: w.at[layer, 0 : len(turns) * ROWS, 0:width], gz_send, unit)

    def gather_direct(unit):
        layer, _start, width, _first, _rows = UNITS[unit]
        arrived(unit_view(unit, slice(0, 7 * ROWS), core), gz_send.at[unit], gz_recv.at[unit])
        ref = unit_view(unit, slice(0, D), core)
        push(ref, ref, gs_send.at[unit], gs_recv.at[unit], sibling)
        sent(gathers, lambda: w.at[layer, :, 0:width], gs_send, unit)

    def gather_z(unit):
        layer, _start, width, _first, _rows = UNITS[unit]
        arrived(unit_view(unit, slice(0, 3 * ROWS), core), gz_send.at[unit], gz_recv.at[unit])
        for part in range(2):
            ref = unit_view(unit, rows_of(dp), core, part)
            where = device(1 - dp, z, (y, 1 - y)[part], x, core)
            push(ref, ref, gy_send.at[unit], gy_recv.at[unit], where)
        sent(gathers, lambda: w.at[layer, 0 : 4 * ROWS, 0:width], gy_send, unit)
        ref = unit_view(unit, rows_of(dp), core)
        push(ref, ref, gs_send.at[unit], gs_recv.at[unit], sibling)

    def gather_y(unit):
        layer, _start, width, _first, _rows = UNITS[unit]
        ref = unit_view(unit, rows_of(1 - dp), core)
        arrived(ref, gy_send.at[unit], gy_recv.at[unit])
        push(ref, ref, gs_send.at[unit], gs_recv.at[unit], sibling)
        sent(gathers, lambda: w.at[layer, :, 0:width], gs_send, unit)

    def gather_end(unit):
        arrived(unit_view(unit, slice(0, D), 1 - core), gs_send.at[unit], gs_recv.at[unit])

    moves = ((acts, img), (cot_in, cot))

    def image_copy(index, entry, home):
        source, target = moves[index]
        return copy_to(
            source.at[entry],
            target.at[image_rows(position), :],
            i_send.at[index],
            i_recv.at[index],
            device(dp, z, y, home // 2, home % 2),
        )

    def image_local(index, entry):
        source, target = moves[index]
        return pltpu.make_async_copy(
            source.at[entry], target.at[image_rows(position), :], i_local.at[index]
        )

    def image_send(index):
        for entry, home in enumerate(OWNERS):

            @pl.when(position != home)
            def _():
                image_copy(index, entry, home).start()

            @pl.when(position == home)
            def _():
                image_local(index, entry).start()

    def image_arrive(index):
        source, target = moves[index]

        @pl.when(jnp.logical_not(owner))
        def _():
            target[...] = jnp.zeros_like(target)
            copy_to(source, source, i_send.at[index], i_recv.at[index], sibling).wait_send()

        @pl.when(owner)
        def _():
            image_local(index, 0).wait()
            ref = source.at[0:5]
            copy_to(ref, ref, i_send.at[index], i_recv.at[index], sibling).wait_send()
            arrived(target.at[0 : 7 * 96, :], i_send.at[index], i_recv.at[index])

    def grad_root(unit):
        return active if UNITS[unit][1] == 0 else w

    def grad_view(unit, rows, side, part=None):
        return grad_root(unit).at[UNITS[unit][0], rows, cols_of(unit, side, part)]

    def reduce_core(unit):
        layer, _start, width, _first, _rows = UNITS[unit]
        root = grad_root(unit)
        for index, side in enumerate((1 - dp, dp)):
            push(
                grad_view(unit, rows_of(side), 1 - core),
                core_buf[unit].at[index],
                rc_send.at[unit],
                rc_recv.at[unit, index],
                sibling,
            )
        sent(reduces, lambda: root.at[layer, 0:D, 0:width], rc_send, unit)

    def reduce_y(unit):
        layer, _start, width, first, _rows = UNITS[unit]
        arrived(core_buf[unit].at[0], rc_send.at[unit], rc_recv.at[unit, 0])

        def add(block, carried):
            ref = grad_view(unit, rows_at((1 - dp) * 4 + block), core)
            ref[...] = (ref[...].astype(F32) + core_buf[unit][0, rows_at(block), :].astype(F32)).astype(BF)
            return carried

        lax.fori_loop(0, 4, add, 0)
        for part, cols in enumerate((slice(0, first), slice(first, width))):
            push(
                grad_view(unit, rows_of(1 - dp), core, part),
                y_buf[unit].at[:, cols],
                ry_send.at[unit],
                ry_recv.at[unit],
                device(1 - dp, z, (y, 1 - y)[part], x, core),
            )
        sent(reduces, lambda: y_buf[unit], ry_send, unit)

    def reduce_z(unit):
        layer, _start, width, first, _rows = UNITS[unit]
        arrived(core_buf[unit].at[1], rc_send.at[unit], rc_recv.at[unit, 1])
        arrived(y_buf[unit], ry_send.at[unit], ry_recv.at[unit])
        for turn in (1, 2, 3, 0):
            block = turned(z, turn, 4)
            ref = grad_view(unit, rows_at(dp * 4 + block), core)
            total = (
                ref[...].astype(F32)
                + core_buf[unit][1, rows_at(block), :].astype(F32)
                + y_buf[unit][rows_at(block), :].astype(F32)
            )
            ref[...] = total.astype(BF)
            if turn:
                push(
                    ref,
                    z_buf[unit].at[turn - 1],
                    rz_send.at[unit],
                    rz_recv.at[unit],
                    device(dp, block, y, x, core),
                )
        sent(reduces, lambda: z_buf[unit], rz_send, unit)

    def reduce_direct(unit):
        layer, _start, width, _first, _rows = UNITS[unit]
        for index in range(2):
            arrived(core_buf[unit].at[index], rc_send.at[unit], rc_recv.at[unit, index])
        for turn in (1, 2, 3, 4, 5, 6, 7, 0):
            to_dp, to_z = turned(dp, turn // 4, 2), turned(z, turn % 4, 4)
            ref = grad_view(unit, rows_at(to_dp * 4 + to_z), core)
            total = ref[...].astype(F32) + core_buf[unit][1 - turn // 4, rows_at(to_z), :].astype(F32)
            ref[...] = total.astype(BF)
            if turn:
                push(
                    ref,
                    z_buf[unit].at[turn - 1],
                    rz_send.at[unit],
                    rz_recv.at[unit],
                    device(to_dp, to_z, y, x, core),
                )
        sent(reduces, lambda: z_buf[unit], rz_send, unit)

    def reduce_slab(unit):
        layer, _start, width, _first, (begin, end) = UNITS[unit]
        total = grad_view(unit, rows_at(dp * 4 + z), core)[...].astype(F32)
        arrived(z_buf[unit], rz_send.at[unit], rz_recv.at[unit])
        for turn in range(1, 8 if unit == 0 else 4):
            total = total + z_buf[unit][turn - 1].astype(F32)
        low = total.astype(BF)
        for group in range((end - begin) // 16):
            parts = [
                low[:, 128 * chunk : 128 * chunk + 128]
                if chunk < width // 128
                else jnp.zeros((ROWS, 128), BF)
                for chunk in range(4 * group, 4 * group + 4)
            ]
            tall = dot_tn(onehot[...], jnp.concatenate(parts, axis=0)).astype(BF)
            at = begin + 16 * group
            slabs[layer, :, at : at + 16, :] = tall.reshape(SPLIT, 16, 128)

    def reduce_plane(group):
        layer, begin, end = GROUPS[group]
        for turn in range(1, 16):
            to_y, to_x, to_core = plane_target(turn)
            push(
                slabs.at[layer, to_y * 8 + to_x * 2 + to_core, begin:end, :],
                ends.at[layer, turn, begin:end, :],
                rp_send.at[group],
                rp_recv.at[group],
                device(dp, z, to_y, to_x, to_core),
            )
        sent(reduces, lambda: slabs.at[layer, 1:16, begin:end, :], rp_send, group)

    outs = ((o_qkv, 0, 9), (o_out, 10, 13), (o_up, 13, 25), (o_down, 25, 37))

    def reduce_end(group):
        layer, begin, end = GROUPS[group]
        totals = [slabs[layer, mine, begin:end, :].astype(F32), None]
        arrived(ends.at[layer, 1:16, begin:end, :], rp_send.at[group], rp_recv.at[group])
        for turn in range(1, 16):
            value = ends[layer, turn, begin:end, :].astype(F32)
            side = turn % 2
            totals[side] = value if totals[side] is None else totals[side] + value
        first = core == 0
        halves = (
            jnp.where(first, totals[0], totals[1]),
            jnp.where(first, totals[1], totals[0]),
        )
        for of, start, width, _first, (low, high) in UNITS:
            for chunk in range(width // 64) if of == layer and begin <= low and high <= end else ():
                inner = low - begin + 4 * (chunk % (width // 128))
                rows = halves[chunk // (width // 128)][inner : inner + 3]
                for target, lowest, highest in outs:
                    if lowest <= start // 128 + chunk < highest:
                        at = 128 * (start // 128 + chunk - lowest)
                        target[:, layer, at : at + 128] = rows

    def misc_out(layer, total):
        tall_sums[...] = jnp.concatenate([total, jnp.zeros((120, D), F32)], axis=0).T
        at = lax.broadcasted_iota(jnp.int32, (8, 128), 0)
        rows = jnp.zeros((8, 128), F32)
        for feature in range(3):
            line = tall_sums[pl.ds(3 * (dp * 64 + sp) + feature, 1), :]
            o_biases[feature, layer : layer + 1, :] = line[:, 2:8]
            rows = jnp.where(at == feature, line, rows)
        wide = jnp.concatenate([rows, jnp.zeros((120, 128), F32)], axis=0).T
        o_gains[layer] = wide[0:2, 0:3]

    def early_sum(stage):
        def send(source, target, where):
            push(source, target, h_send.at[stage], h_recv.at[stage], where)

        def wait(ref):
            arrived(ref, h_send.at[stage - 1], h_recv.at[stage - 1])

        if stage == 0:
            for layer in range(LAYERS):
                early[3 * layer : 3 * layer + 3, :] = hid_sums[layer]
            early[8:16, 0:D] = row_sums[1]
            send(early, h_core, sibling)
            sent(reduces, lambda: early, h_send, 0)
        elif stage == 1:
            wait(h_core)
            h_sum[0] = early[...] + h_core[...]
            send(h_sum.at[0], h_y, device(1 - dp, z, y, x, core))
            sent(reduces, lambda: early, h_send, 1)
        elif stage == 2:
            wait(h_y)
            h_sum[1] = h_sum[0] + h_y[...]
            for turn in range(1, 4):
                send(h_sum.at[1], h_z.at[turn - 1], device(dp, turned(z, turn, 4), y, x, core))
            sent(reduces, lambda: h_z, h_send, 2)
        elif stage == 3:
            wait(h_z)
            h_sum[2] = h_sum[1] + h_z[0] + h_z[1] + h_z[2]
            for turn in range(1, 8):
                where = device(dp, z, turned(y, turn // 4, 2), turned(x, turn % 4, 4), core)
                send(h_sum.at[2], h_p.at[turn], where)
            sent(reduces, lambda: h_p.at[1:8], h_send, 3)
        else:
            wait(h_p.at[1:8])
            total = h_sum[2]
            for turn in range(1, 8):
                total = total + h_p[turn]
            for layer in range(LAYERS):
                for chunk in range(FF // FC):
                    hid[layer, :, FC * chunk : FC * chunk + FC] = total[
                        3 * layer + chunk : 3 * layer + chunk + 1
                    ]
            for layer in range(LAYERS):
                share = pl.ds(pl.multiple_of(dp * (FF // 2), 128), FF // 2)
                o_hid[layer : layer + 1, :] = hid[layer, :, share]
            misc_out(1, total[8:16, 0:D])

    def late_sum(stage):
        if stage == 0:
            late[...] = row_sums[0]
            for turn in range(1, 16):
                where = device(dp, z, *plane_target(turn))
                push(late, l_plane.at[turn], l_send.at[0], l_recv.at[0], where)
            sent(reduces, lambda: l_plane.at[1:16], l_send, 0)
        elif stage == 1:
            arrived(l_plane.at[1:16], l_send.at[0], l_recv.at[0])
            total = late[...]
            for turn in range(1, 16):
                total = total + l_plane[turn]
            l_sum[...] = total
            for turn in range(1, 8):
                where = device(turned(dp, turn // 4, 2), turned(z, turn % 4, 4), y, x, core)
                push(l_sum, l_far.at[turn], l_send.at[1], l_recv.at[1], where)
            sent(reduces, lambda: l_far.at[1:8], l_send, 1)
        else:
            arrived(l_far.at[1:8], l_send.at[1], l_recv.at[1])
            total = l_sum[...]
            for turn in range(1, 8):
                total = total + l_far[turn]
            misc_out(0, total)

    backs = ((act, act_out), (igrad, igrad_out))

    def back_copy(index, home):
        source, target = backs[index]
        return copy_to(
            source.at[96 * home : 96 * home + 96, :],
            target.at[entry_mine],
            e_send.at[index],
            e_recv.at[index],
            device(dp, z, y, home // 2, home % 2),
        )

    def back_local(index, home):
        source, target = backs[index]
        return pltpu.make_async_copy(
            source.at[96 * home : 96 * home + 96, :], target.at[entry_mine], e_local.at[index]
        )

    def back_send(index, first, last):
        for home in range(first, last):

            @pl.when(jnp.logical_and(owner, position != home))
            def _():
                back_copy(index, home).start()

            @pl.when(jnp.logical_and(owner, position == home))
            def _():
                back_local(index, home).start()

    def back_arrive(index):
        source, target = backs[index]

        @pl.when(owner)
        def _():
            back_local(index, 0).wait()
            ref = source.at[0 : 7 * 96, :]
            copy_to(ref, ref, e_send.at[index], e_recv.at[index], sibling).wait_send()
            arrived(target.at[0:5], e_send.at[index], e_recv.at[index])

        @pl.when(jnp.logical_not(owner))
        def _():
            arrived(target, e_send.at[index], e_recv.at[index])

    length = lengths[jnp.minimum(entry_mine, 5), lax.div(dp * 64 + sp, 8)]
    (
        project, attend, feed, turn_back, unfeed, feed_grads, unproject_out, unattend, qkv_grads, unproject,
    ) = encoder(
        length, w, carry, inputs, cot, act, igrad, hid, hid_sums, row_sums,
        mids, qkv, probs_even, probs_odd, invs, att, att_low, active, slope, low_a, low_b, dqkv, trans, trans_b, prm,
    )

    def run(layer, *steps):
        for of in range(LAYERS):
            chosen = [step for step in steps if step[0] == of]
            if chosen:

                @pl.when(layer == of)
                def _():
                    for _of, function, *arguments in chosen:
                        function(*arguments)

    def pairs(body, layer, hooks):
        def one(pair, carried):
            body(layer, pair)
            for at, of, function, *arguments in hooks:

                @pl.when(jnp.logical_and(pair == at, layer == of))
                def _():
                    function(*arguments)

            return carried

        lax.fori_loop(0, PAIRS, one, 0)

    def hidden_arrive():
        arrived(hid_all.at[1 - dp], b_send.at[0], b_recv.at[0])
        for side in range(2):
            for layer in range(LAYERS):
                hid[layer, :, side * (FF // 2) : (side + 1) * (FF // 2)] = hid_all[side, layer : layer + 1, :]

    slab_send(0)
    image_send(0)
    slab_send(1)
    slab_build_layer(1)
    hid_all[dp] = p_hid[...].astype(F32)
    push(hid_all.at[dp], hid_all.at[dp], b_send.at[0], b_recv.at[0], device(1 - dp, z, y, x, core))
    sent(gathers, lambda: hid_all.at[0], b_send, 0)
    onehot[...] = spread_matrix()
    invs[...] = jnp.zeros_like(invs)
    hid_sums[...] = jnp.zeros_like(hid_sums)
    row_sums[...] = jnp.zeros_like(row_sums)
    early[...] = jnp.zeros_like(early)
    slab_arrive(0)
    block_build(0)
    slab_send(2)
    slab_arrive(1)
    block_build(1)
    block_build(2)
    gather_direct(0)
    gather_z(1)
    slab_arrive(2)
    block_build(3)
    block_build(4)
    image_arrive(0)
    carry[...] = img[...].astype(F32)
    gather_z(2)
    gather_end(0)

    def forward(layer, carried):
        project(layer)
        run(layer, (0, gather_y, 1))
        pairs(
            attend,
            layer,
            ((0, 0, gather_z, 3), (0, 0, image_send, 1), (1, 0, gather_y, 2), (1, 1, gather_y, 4)),
        )
        run(
            layer,
            (0, gather_z, 4),
            (0, gather_y, 3),
            (0, hidden_arrive),
            (0, gather_end, 1),
            (0, gather_end, 2),
            (1, gather_end, 4),
        )
        feed(layer)
        run(layer, (0, gather_end, 3))
        return carried

    lax.fori_loop(0, LAYERS, forward, 0)
    back_send(0, 0, 8)
    image_arrive(1)
    turn_back()
    all_sent(gathers)

    def backward(step, carried):
        layer = LAYERS - 1 - step
        unfeed(layer)
        run(layer, (0, early_sum, 0), (0, reduce_z, 4), (0, reduce_y, 3))
        feed_grads(layer)
        run(layer, (0, reduce_core, 2))
        unproject_out(layer)
        run(
            layer,
            (1, reduce_core, 4),
            (0, reduce_core, 1),
            (0, early_sum, 1),
            (0, reduce_z, 3),
            (0, reduce_y, 2),
        )
        pairs(
            unattend,
            layer,
            (
                (0, 0, reduce_y, 1),
                (1, 0, early_sum, 2),
                (1, 0, reduce_slab, 4),
                (1, 0, reduce_z, 2),
                (1, 1, reduce_y, 4),
                (2, 0, reduce_z, 1),
            ),
        )
        run(layer, (0, reduce_slab, 3), (0, reduce_plane, 2), (0, early_sum, 3))
        qkv_grads(layer)
        run(layer, (1, reduce_core, 3), (0, reduce_core, 0))
        unproject(layer, lambda: run(layer, (0, back_send, 1, 0, 4), (0, reduce_direct, 0)))
        return carried

    lax.fori_loop(0, LAYERS, backward, 0)
    late_sum(0)
    back_send(1, 4, 8)
    early_sum(4)
    late_sum(1)
    reduce_end(2)
    reduce_slab(2)
    reduce_slab(1)
    reduce_plane(1)
    reduce_slab(0)
    reduce_plane(0)
    late_sum(2)
    reduce_end(1)
    for index in range(2):
        back_arrive(index)
    reduce_end(0)
    all_sent(reduces)


def finish_kernel(
    i_qkv, i_out, i_up, i_down, i_gains, i_biases, i_hid, i_act, i_igrad,
    act, igrad, g_qkv, g_out, g_up, g_down, g_gains, g_biases, g_hid,
):
    act[...] = i_act[...].astype(F32)
    igrad[...] = i_igrad[...].astype(F32)
    for source, target in (
        (i_qkv, g_qkv),
        (i_out, g_out),
        (i_up, g_up),
        (i_down, g_down),
        (i_gains, g_gains),
        (i_biases, g_biases),
        (i_hid, g_hid),
    ):
        target[...] = source[...]


def local(acts, cotangent, lengths, w_qkv, w_out, w_up, w_down, gains, biases, hidden_bias):
    swap = lambda array: array.transpose(1, 0, 2)
    vmem = pl.BlockSpec(memory_space=pltpu.VMEM)
    any_space = pl.BlockSpec(memory_space=pl.ANY)
    shape = jax.ShapeDtypeStruct
    buffer = pltpu.VMEM
    dma = pltpu.SemaphoreType.DMA
    pair = lambda *dims: [dma(dims), dma(dims)]
    results = pl.pallas_call(
        kernel,
        out_shape=(
            shape((3, LAYERS, 3 * D), F32),
            shape((3, LAYERS, D), F32),
            shape((3, LAYERS, FF), F32),
            shape((3, LAYERS, FF), F32),
            shape((LAYERS, 2, 3), F32),
            shape((3, LAYERS, 6), F32),
            shape((LAYERS, FF // 2), F32),
            shape((6, 96, D), BF),
            shape((6, 96, D), BF),
        ),
        in_specs=[pl.BlockSpec(memory_space=pltpu.SMEM), any_space, any_space] + [vmem] * 7,
        out_specs=(vmem,) * 7 + (any_space,) * 2,
        scratch_shapes=[
            buffer((LAYERS, D, WIDE), BF),
            buffer((TOK, D), F32),
            buffer((LAYERS, TOK, D), F32),
            buffer((TOK, D), BF),
            buffer((TOK, D), BF),
            buffer((TOK, D), BF),
            buffer((4 * ROWS, 256), BF),
            buffer((SLAB, 128), F32),
            buffer((2, LAYERS, FF // 2), F32),
            buffer((LAYERS, 1, FF), F32),
            buffer((LAYERS, 3, FC), F32),
            buffer((LAYERS, 8, D), F32),
            buffer((16, FC), F32),
            buffer((8, D), F32),
            buffer((D, 128), F32),
            *compute_scratch(),
            buffer((LAYERS, 2, SLAB, 128), BF),
            buffer((LAYERS, SPLIT, SLAB, 128), BF),
            buffer((LAYERS, SPLIT, SLAB, 128), BF),
            buffer((LAYERS, SPLIT, SLAB, 128), BF),
            buffer((16, FC), F32),
            buffer((16, FC), F32),
            buffer((3, 16, FC), F32),
            buffer((8, 16, FC), F32),
            buffer((3, 16, FC), F32),
            buffer((16, 8, D), F32),
            buffer((8, 8, D), F32),
            buffer((8, D), F32),
        ]
        + pair(len(GROUPS))
        + pair(COUNT)
        + pair(COUNT)
        + pair(COUNT)
        + [dma((2,)), dma((2,)), dma((2,)), dma((1,)), dma((1,))]
        + [dma((COUNT,)), dma((COUNT, 2))]
        + pair(COUNT)
        + pair(COUNT)
        + pair(len(GROUPS))
        + [dma((2,)), dma((2,)), dma((2,))]
        + pair(4)
        + pair(2)
        + [buffer((2, 4 * ROWS, unit[2]), BF) for unit in UNITS]
        + [buffer((4 * ROWS if index else 16, unit[2]), BF) for index, unit in enumerate(UNITS)]
        + [buffer((3 if index else 7, ROWS, unit[2]), BF) for index, unit in enumerate(UNITS)],
        compiler_params=pltpu.CompilerParams(
            collective_id=0, has_side_effects=True, vmem_limit_bytes=63 * MIB
        ),
        name="encoder",
    )(
        lengths, acts, cotangent, swap(w_qkv), swap(w_out), swap(w_up), swap(w_down),
        gains.transpose(0, 2, 1), swap(biases), hidden_bias,
    )
    act, igrad, g_qkv, g_out, g_up, g_down, g_gains, g_biases, g_hid = pl.pallas_call(
        finish_kernel,
        out_shape=(
            shape((6, 96, D), F32),
            shape((6, 96, D), F32),
            shape((3, LAYERS, 3 * D), F32),
            shape((3, LAYERS, D), F32),
            shape((3, LAYERS, FF), F32),
            shape((3, LAYERS, FF), F32),
            shape((LAYERS, 2, 3), F32),
            shape((3, LAYERS, 6), F32),
            shape((LAYERS, FF // 2), F32),
        ),
        in_specs=[vmem] * 9,
        out_specs=(vmem,) * 9,
        name="finish",
    )(*results)
    return (
        act,
        igrad,
        swap(g_qkv),
        swap(g_out),
        swap(g_up),
        swap(g_down),
        g_gains.transpose(0, 2, 1),
        swap(g_biases),
        g_hid,
    )


def solution(mesh):
    split = P(None, ("dp", "sp"), None)
    return jax.shard_map(
        local,
        mesh=mesh,
        in_specs=(split, split, P(), split, split, split, split, split, split, P(None, "dp")),
        out_specs=(split,) * 8 + (P(None, "dp"),),
        check_vma=False,
    )
```

```python
import math

import jax
import jax.numpy as jnp
from jax import lax
from jax.experimental import pallas as pl
from jax.experimental.pallas import tpu as pltpu
from jax.sharding import PartitionSpec as P

D = 384
HEADS = 6
PAIRS = HEADS // 2
HEAD_DIM = 64
FF = 1536
LAYERS = 2
TOK = 768
EPSILON = 1e-06
NEG_FILL = -1e30
GELU_COEF = math.sqrt(2.0 / math.pi)
CUBIC_COEF = 0.044715
BF = jnp.bfloat16
F32 = jnp.float32
RB = 384
FC = 512
MIB = 1024 * 1024

MISC0, OUT0, UP0, DOWN0, WIDE = 1152, 1280, 1664, 3200, 4864
UNITS = (
    (0, 0, 640, 384, (0, 32)),
    (0, 1280, 896, 384, (32, 64)),
    (0, 3072, 896, 384, (64, 96)),
    (1, 0, 640, 384, (0, 32)),
    (1, 1280, 1792, 896, (32, 96)),
)
COUNT = len(UNITS)
SLAB = 96
GROUPS = ((0, 0, 32), (0, 32, 96), (1, 0, 96))

OWNERS = (0, 1, 2, 4, 5, 6)
MESH = pl.DeviceIdType.MESH
SPLIT = 16
ROWS = 48


def dot(left_side, right_side):
    return jnp.dot(left_side, right_side, preferred_element_type=F32)


def dot_nt(left_side, right_side):
    return lax.dot_general(
        left_side, right_side, (((1,), (1,)), ((), ())), preferred_element_type=F32
    )


def dot_tn(left_side, right_side):
    return lax.dot_general(
        left_side, right_side, (((0,), (0,)), ((), ())), preferred_element_type=F32
    )


def normalized(values):
    center = values - jnp.mean(values, axis=-1, keepdims=True)
    inverse = lax.rsqrt(jnp.mean(center * center, axis=-1, keepdims=True) + EPSILON)
    return center * inverse, inverse


def norm_backward(upstream, xhat, inverse, gain):
    scaled = upstream * gain
    return inverse * (
        scaled
        - jnp.mean(scaled, axis=-1, keepdims=True)
        - xhat * jnp.mean(scaled * xhat, axis=-1, keepdims=True)
    )


def gelu_pair(hidden):
    square = hidden * hidden
    tangent = jnp.tanh(hidden * (GELU_COEF + (GELU_COEF * CUBIC_COEF) * square))
    half = 0.5 + 0.5 * tangent
    active = hidden * half
    slope = half + active * (1.0 - tangent) * (
        GELU_COEF + (3.0 * GELU_COEF * CUBIC_COEF) * square
    )
    return active, slope


def colsum(values):
    return jnp.sum(values.astype(F32), axis=0, keepdims=True)


def each_block(body):
    for start in range(0, TOK, RB):
        body(slice(start, start + RB))


def each_chunk(stop, width, body):
    for start in range(0, stop, width):
        body(slice(start, start + width), lambda base, at=start: slice(base + at, base + at + width))


def encoder(
    length, w, carry, inputs, cot, act, igrad, hid, hid_sums, row_sums,
    mids, qkv, probs_even, probs_odd, invs, att, att_low, active, slope, low_a, low_b, dqkv, trans, trans_b, prm,
):
    last_valid = lax.broadcasted_iota(jnp.int32, (1, 128), 1) + (TOK - 128) < length
    lanes = lax.broadcasted_iota(jnp.int32, (1, 128), 1)
    first_half = lanes < 64
    scale = HEAD_DIM ** (-0.5)

    def lanes_at(pair, base):
        return pl.ds(pl.multiple_of(base + 128 * pair, 128), 128)

    def half_of(block, which):
        keep = first_half if which == 0 else jnp.logical_not(first_half)
        return jnp.where(keep, block, jnp.zeros_like(block))

    def row(layer, index):
        at = (index + 6) % 8
        return prm[layer, at : at + 1, :]

    def project(layer):
        prm[layer] = w[layer, :, MISC0 : MISC0 + 128].astype(F32).T[0:8]

        bias = jnp.concatenate([row(layer, 2), jnp.zeros((1, D), F32), row(layer, 3)], axis=1)

        def body(rows):
            source = carry[rows, :]
            inputs[layer, rows, :] = source
            xhat, _inverse = normalized(source)
            low = (xhat * row(layer, 0) + row(layer, 5)).astype(BF)
            qkv[layer, rows, :] = (dot(low, w[layer, :, 0 : 3 * D]) + bias).astype(BF)

        each_block(body)
        trans[...] = qkv[layer, :, D : 2 * D].T

    def attend(layer, pair):
        lane = lanes_at(pair, 0)
        value = qkv[layer, :, lanes_at(pair, 2 * D)]
        value = jnp.concatenate([value, jnp.ones((TOK, 128), BF)], axis=1)

        def body(rows):
            query = qkv[layer, rows, lane] * jnp.asarray(scale, BF)
            results = []
            kept = invs[rows, :]
            for which in range(2):
                head = 2 * pair + which
                scores = dot(half_of(query, which), trans[lane, :])
                last = jnp.where(last_valid, scores[:, TOK - 128 :], NEG_FILL)
                scores = jnp.concatenate([scores[:, : TOK - 128], last], axis=1)
                low = jnp.exp(scores - jnp.max(scores, axis=-1, keepdims=True)).astype(BF)
                (probs_even, probs_odd)[which][layer, pair, rows, :] = low
                product = dot(low, value)
                inverse = 1.0 / product[:, 128:]
                results.append(product[:, :128] * inverse)
                kept = jnp.where(lanes == 8 * layer + head, inverse, kept)
            invs[rows, :] = kept
            whole = jnp.where(first_half, results[0], results[1])
            high = whole.astype(BF)
            att[layer, rows, lane] = high
            att_low[layer, rows, lane] = (whole - high.astype(F32)).astype(BF)

        each_block(body)

    def feed(layer):
        def body(rows):
            mid = inputs[layer, rows, :] + (
                dot(att[layer, rows, :], w[layer, :, OUT0 : OUT0 + D]) + row(layer, 4)
            )
            mids[layer, rows, :] = mid
            xhat, _inverse = normalized(mid)
            low = (xhat * row(layer, 1) + row(layer, 6)).astype(BF)
            total = mid + row(layer, 7)
            for chunk in range(FF // FC):
                cols = slice(FC * chunk, FC * chunk + FC)
                hidden = dot(low, w[layer, :, UP0 + FC * chunk : UP0 + FC * chunk + FC])
                value, rate = gelu_pair(hidden + hid[layer, :, cols])
                value = value.astype(BF)
                active[layer, rows, cols] = value
                slope[layer, rows, cols] = rate.astype(BF)
                total = total + dot_nt(
                    value, w[layer, :, DOWN0 + FC * chunk : DOWN0 + FC * chunk + FC]
                )
            carry[rows, :] = total
            act[rows, :] = total.astype(BF)

        each_block(body)

    def add_sum(layer, index, values):
        row_sums[layer, index : index + 1, :] += colsum(values)

    def turn_back():
        carry[...] = cot[...].astype(F32)

    def unfeed(layer):
        def body(rows):
            upstream = carry[rows, :]
            down = upstream.astype(BF)
            low_a[rows, :] = down
            add_sum(layer, 7, down)
            xhat, inverse = normalized(mids[layer, rows, :])
            low_b[rows, :] = (xhat * row(layer, 1) + row(layer, 6)).astype(BF)
            total = jnp.zeros((RB, D), F32)
            for chunk in range(FF // FC):
                cols = slice(FC * chunk, FC * chunk + FC)
                grad = dot(down, w[layer, :, DOWN0 + FC * chunk : DOWN0 + FC * chunk + FC])
                grad = (grad * slope[layer, rows, cols].astype(F32)).astype(BF)
                slope[layer, rows, cols] = grad
                hid_sums[layer, chunk : chunk + 1, :] += colsum(grad)
                total = total + dot_nt(grad, w[layer, :, UP0 + FC * chunk : UP0 + FC * chunk + FC])
            add_sum(layer, 1, total * xhat)
            add_sum(layer, 6, total)
            carry[rows, :] = upstream + norm_backward(total, xhat, inverse, row(layer, 1))

        each_block(body)

    def feed_grads(layer):
        trans[...] = low_a[...].T
        trans_b[...] = low_b[...].T

        def grad_down(cols, at):
            w[layer, :, at(DOWN0)] = dot(trans[...], active[layer, :, cols]).astype(BF)

        def grad_up(cols, at):
            w[layer, :, at(UP0)] = dot(trans_b[...], slope[layer, :, cols]).astype(BF)

        each_chunk(FF, FC, grad_down)
        each_chunk(FF, FC, grad_up)

    def unproject_out(layer):
        def body(rows):
            low = carry[rows, :].astype(BF)
            low_a[rows, :] = low
            add_sum(layer, 4, low)
            grad = dot_nt(low, w[layer, :, OUT0 : OUT0 + D])
            inverse = jnp.where(layer == 0, invs[rows, 0:8], invs[rows, 8:16])
            for pair in range(PAIRS):
                lane = slice(128 * pair, 128 * pair + 128)
                both = jnp.where(
                    first_half,
                    inverse[:, 2 * pair : 2 * pair + 1],
                    inverse[:, 2 * pair + 1 : 2 * pair + 2],
                )
                low_b[rows, lane] = (grad[:, lane] * both).astype(BF)

        each_block(body)
        trans[...] = att[layer].T
        w[layer, :, OUT0 : OUT0 + D] = dot(trans[...], low_a[...]).astype(BF)
        trans[...] = low_b[...].T
        trans_b[...] = (qkv[layer, :, 0:D] * jnp.asarray(scale, BF)).T

    def unattend(layer, pair):
        lane = lanes_at(pair, 0)
        key = qkv[layer, :, lanes_at(pair, D)]
        value = qkv[layer, :, lanes_at(pair, 2 * D)]
        key_parts, value_parts = [0.0, 0.0], [0.0, 0.0]

        def body(rows):
            grad = low_b[rows, lane]
            whole = att[layer, rows, lane].astype(F32) + att_low[layer, rows, lane].astype(F32)
            weighted = grad.astype(F32) * whole
            results = []
            for which, probs in enumerate((probs_even, probs_odd)):
                feature = pl.ds(pl.multiple_of(128 * pair + 64 * which, 64), 64)
                low = probs[layer, pair, rows, :]
                inner = jnp.sum(half_of(weighted, which), axis=-1, keepdims=True)
                prob_grad = dot_nt(half_of(grad, which), value)
                score_grad = (low.astype(F32) * (prob_grad - inner)).astype(BF)
                results.append(dot(score_grad, key))
                key_parts[which] += dot(trans_b[feature, rows], score_grad)
                value_parts[which] += dot(trans[feature, rows], low)
            dqkv[rows, lane] = (jnp.where(first_half, results[0], results[1]) * scale).astype(BF)

        each_block(body)
        dqkv[:, lanes_at(pair, D)] = jnp.concatenate(key_parts, axis=0).T.astype(BF)
        dqkv[:, lanes_at(pair, 2 * D)] = jnp.concatenate(value_parts, axis=0).T.astype(BF)

    def qkv_grads(layer):
        def body(rows):
            xhat, _inverse = normalized(inputs[layer, rows, :])
            low_a[rows, :] = (xhat * row(layer, 0) + row(layer, 5)).astype(BF)

        each_block(body)
        trans[...] = low_a[...].T

        def grad_qkv(cols, _at):
            active[layer, 0:D, cols] = dot(trans[...], dqkv[:, cols]).astype(BF)

        each_chunk(3 * D, D, grad_qkv)

    def unproject(layer, between):
        def body(rows):
            if rows.stop == TOK:
                between()
            add_sum(layer, 2, dqkv[rows, 0:D])
            add_sum(layer, 3, dqkv[rows, 2 * D : 3 * D])
            xhat, inverse = normalized(inputs[layer, rows, :])
            total = dot_nt(dqkv[rows, :], w[layer, :, 0 : 3 * D])
            add_sum(layer, 0, total * xhat)
            add_sum(layer, 5, total)
            upstream = carry[rows, :] + norm_backward(total, xhat, inverse, row(layer, 0))
            carry[rows, :] = upstream
            igrad[rows, :] = upstream.astype(BF)

        each_block(body)

    return (
        project, attend, feed, turn_back, unfeed, feed_grads, unproject_out, unattend, qkv_grads, unproject,
    )


def compute_scratch():
    return [
        pltpu.VMEM((LAYERS, TOK, D), F32),
        pltpu.VMEM((LAYERS, TOK, 3 * D), BF),
        pltpu.VMEM((LAYERS, PAIRS, TOK, TOK), BF),
        pltpu.VMEM((LAYERS, PAIRS, TOK, TOK), BF),
        pltpu.VMEM((TOK, 128), F32),
        pltpu.VMEM((LAYERS, TOK, D), BF),
        pltpu.VMEM((LAYERS, TOK, D), BF),
        pltpu.VMEM((LAYERS, TOK, FF), BF),
        pltpu.VMEM((LAYERS, TOK, FF), BF),
        pltpu.VMEM((TOK, D), BF),
        pltpu.VMEM((TOK, 3 * D), BF),
        pltpu.VMEM((D, TOK), BF),
        pltpu.VMEM((D, TOK), BF),
        pltpu.VMEM((LAYERS, 8, D), F32),
    ]


def device(dp, z, y, x, core):
    return (dp, z * 16 + y * 8 + x * 2 + core)


def turned(value, by, count):
    return lax.rem(value + (by + count), count)


def rows_at(block):
    return pl.ds(pl.multiple_of(block * ROWS, 16), ROWS)


def image_rows(position):
    return pl.ds(pl.multiple_of(position * 96, 16), 96)


def copy_to(source, target, send, recv, where):
    return pltpu.make_async_remote_copy(
        src_ref=source,
        dst_ref=target,
        send_sem=send,
        recv_sem=recv,
        device_id=where,
        device_id_type=MESH,
    )


def spread_matrix():
    out = lax.broadcasted_iota(jnp.int32, (4 * ROWS, 256), 0)
    col = lax.broadcasted_iota(jnp.int32, (4 * ROWS, 256), 1)
    member, inner, row = col >> 4, (col >> 2) & 3, col & 3
    hit = jnp.logical_and(out == ROWS * inner + 3 * member + row, row < 3)
    return jnp.where(hit, 1.0, 0.0).astype(BF)


def kernel(
    lengths, acts, cot_in, p_qkv, p_out, p_up, p_down, p_gains, p_biases, p_hid,
    o_qkv, o_out, o_up, o_down, o_gains, o_biases, o_hid, act_out, igrad_out,
    w, carry, inputs, img, cot, act, onehot, slab_build, hid_all, hid, hid_sums, row_sums, early, late, tall_sums,
    mids, qkv, probs_even, probs_odd, invs, att, att_low, active, slope, low_b, dqkv, trans, trans_b, prm,
    give, held, slabs, ends,
    h_core, h_y, h_z, h_p, h_sum, l_plane, l_far, l_sum,
    ga_send, ga_recv, gz_send, gz_recv, gy_send, gy_recv, gs_send, gs_recv,
    i_send, i_recv, i_local, b_send, b_recv,
    rc_send, rc_recv, ry_send, ry_recv, rz_send, rz_recv, rp_send, rp_recv,
    e_send, e_recv, e_local, h_send, h_recv, l_send, l_recv,
    *buffers,
):
    core_buf, y_buf, z_buf = [buffers[COUNT * kind : COUNT * kind + COUNT] for kind in range(3)]
    dp, sp = lax.axis_index("dp"), lax.axis_index("sp")
    z = lax.div(sp, 16)
    y = lax.rem(lax.div(sp, 8), 2)
    x = lax.rem(lax.div(sp, 2), 4)
    core = lax.rem(sp, 2)
    mine = y * 8 + x * 2 + core
    position = x * 2 + core
    entry_mine = position - lax.div(position, 4)
    owner = lax.rem(position, 4) < 3
    sibling = device(dp, z, y, x, 1 - core)
    igrad = img
    low_a = cot
    gathers, reduces = [], []

    def push(source, target, send, recv, where):
        copy_to(source, target, send, recv, where).start()

    def all_sent(steps):
        for view, sem, index in steps:
            ref, sem = view(), sem.at[index]
            copy_to(ref, ref, sem, sem, sibling).wait_send()

    def sent(steps, view, sem, *index):
        steps.append((view, sem, index))

    def arrived(ref, send, recv):
        copy_to(ref, ref, send, recv, sibling).wait_recv()

    peers = [sibling]
    for step in range(1, 4):
        peers.append(device(dp, z, y, turned(x, step, 4), core))
        peers.append(device(dp, z, y, turned(x, step, 4), 1 - core))
        peers.append(device(dp, turned(z, step, 4), y, x, core))
        peers.append(device(1 - dp, turned(z, step, 4), y, x, core))
    for step in range(4):
        peers.append(device(dp, z, 1 - y, turned(x, step, 4), core))
        peers.append(device(dp, z, 1 - y, turned(x, step, 4), 1 - core))
    for side in (y, 1 - y):
        peers.append(device(1 - dp, z, side, x, core))
    barrier = pltpu.get_barrier_semaphore()
    for peer in peers:
        pl.semaphore_signal(barrier, inc=1, device_id=peer, device_id_type=MESH)

    def misc_rows(layer):
        slab_build[0:8, :] = jnp.zeros((8, 128), F32)
        slab_build[0:3, 0:6] = p_biases[...].astype(F32)[:, layer, :]
        rows = slab_build[0:3, :]
        at = lax.broadcasted_iota(jnp.int32, (3, 128), 0)
        lane = lax.broadcasted_iota(jnp.int32, (3, 128), 1)
        gains = p_gains[...].astype(F32)
        for gain in range(2):
            for feature in range(3):
                hit = jnp.logical_and(at == feature, lane == 6 + gain)
                rows = jnp.where(hit, gains[layer, gain : gain + 1, feature : feature + 1], rows)
        return rows

    def slab_build_layer(layer):
        whole = jnp.concatenate(
            [p_qkv[...].astype(F32)[:, layer, :], misc_rows(layer)]
            + [ref[...].astype(F32)[:, layer, :] for ref in (p_out, p_up, p_down)]
            + [jnp.zeros((3, 128), F32)],
            axis=1,
        )
        for side in range(2):
            slab_build[...] = jnp.zeros_like(slab_build)
            for of, start, width, _first, rows in UNITS:
                for chunk in range(width // 128) if of == layer else ():
                    at = start + side * width + 128 * chunk
                    row = rows[0] + 4 * chunk
                    slab_build[row : row + 3, :] = whole[:, at : at + 128]
            give[layer, side] = slab_build[...].astype(BF)

    slab_build_layer(0)
    pl.semaphore_wait(barrier, len(peers))

    def plane_target(turn):
        return turned(y, turn // 8, 2), turned(x, turn // 2 % 4, 4), turned(core, turn % 2, 2)

    def plane_source(turn):
        return (
            turned(y, -(turn // 8), 2) * 8
            + turned(x, -(turn // 2 % 4), 4) * 2
            + turned(core, -(turn % 2), 2)
        )

    def slab_send(group):
        layer, begin, end = GROUPS[group]
        held[layer, mine, begin:end, :] = give[layer, core, begin:end, :]
        for turn in range(1, 16):
            to_y, to_x, to_core = plane_target(turn)
            push(
                give.at[layer, to_core, begin:end, :],
                held.at[layer, mine, begin:end, :],
                ga_send.at[group],
                ga_recv.at[group],
                device(dp, z, to_y, to_x, to_core),
            )
        sent(gathers, lambda: held.at[layer, 1:16, begin:end, :], ga_send, group)

    def slab_arrive(group):
        layer, begin, end = GROUPS[group]
        arrived(held.at[layer, 1:16, begin:end, :], ga_send.at[group], ga_recv.at[group])

    def cols_of(unit, side, part):
        _layer, start, width, first, _rows = UNITS[unit]
        begin, count = ((0, width), (0, first), (first, width - first))[0 if part is None else part + 1]
        return pl.ds(pl.multiple_of(start + side * width + begin, 128), count)

    def unit_view(unit, rows, side, part=None):
        return w.at[UNITS[unit][0], rows, cols_of(unit, side, part)]

    def rows_of(side):
        return pl.ds(pl.multiple_of(side * (4 * ROWS), 16), 4 * ROWS)

    def block_build(unit):
        layer, start, width, _first, (begin, end) = UNITS[unit]
        block = rows_at(dp * 4 + z)
        for group in range((end - begin) // 16):
            at = begin + 16 * group
            tall = held[layer, :, at : at + 16, :].reshape(256, 128)
            wide = dot(onehot[...], tall).astype(BF)
            for inner in range(4):
                chunk = 4 * group + inner
                if chunk < width // 128:
                    cols = pl.ds(pl.multiple_of(start + core * width + 128 * chunk, 128), 128)
                    w[layer, block, cols] = wide[ROWS * inner : ROWS * inner + ROWS]
        ref = unit_view(unit, block, core)
        turns = range(1, 8 if unit == 0 else 4)
        for turn in turns:
            where = device(turned(dp, turn // 4, 2), turned(z, turn % 4, 4), y, x, core)
            push(ref, ref, gz_send.at[unit], gz_recv.at[unit], where)
        sent(gathers, lambda: w.at[layer, 0 : len(turns) * ROWS, 0:width], gz_send, unit)

    def gather_direct(unit):
        layer, _start, width, _first, _rows = UNITS[unit]
        arrived(unit_view(unit, slice(0, 7 * ROWS), core), gz_send.at[unit], gz_recv.at[unit])
        ref = unit_view(unit, slice(0, D), core)
        push(ref, ref, gs_send.at[unit], gs_recv.at[unit], sibling)
        sent(gathers, lambda: w.at[layer, :, 0:width], gs_send, unit)

    def gather_z(unit):
        layer, _start, width, _first, _rows = UNITS[unit]
        arrived(unit_view(unit, slice(0, 3 * ROWS), core), gz_send.at[unit], gz_recv.at[unit])
        for part in range(2):
            ref = unit_view(unit, rows_of(dp), core, part)
            where = device(1 - dp, z, (y, 1 - y)[part], x, core)
            push(ref, ref, gy_send.at[unit], gy_recv.at[unit], where)
        sent(gathers, lambda: w.at[layer, 0 : 4 * ROWS, 0:width], gy_send, unit)
        ref = unit_view(unit, rows_of(dp), core)
        push(ref, ref, gs_send.at[unit], gs_recv.at[unit], sibling)

    def gather_y(unit):
        layer, _start, width, _first, _rows = UNITS[unit]
        ref = unit_view(unit, rows_of(1 - dp), core)
        arrived(ref, gy_send.at[unit], gy_recv.at[unit])
        push(ref, ref, gs_send.at[unit], gs_recv.at[unit], sibling)
        sent(gathers, lambda: w.at[layer, :, 0:width], gs_send, unit)

    def gather_end(unit):
        arrived(unit_view(unit, slice(0, D), 1 - core), gs_send.at[unit], gs_recv.at[unit])

    moves = ((acts, img), (cot_in, cot))

    def image_copy(index, entry, home):
        source, target = moves[index]
        return copy_to(
            source.at[entry],
            target.at[image_rows(position), :],
            i_send.at[index],
            i_recv.at[index],
            device(dp, z, y, home // 2, home % 2),
        )

    def image_local(index, entry):
        source, target = moves[index]
        return pltpu.make_async_copy(
            source.at[entry], target.at[image_rows(position), :], i_local.at[index]
        )

    def image_send(index):
        for entry, home in enumerate(OWNERS):

            @pl.when(position != home)
            def _():
                image_copy(index, entry, home).start()

            @pl.when(position == home)
            def _():
                image_local(index, entry).start()

    def image_arrive(index):
        source, target = moves[index]

        @pl.when(jnp.logical_not(owner))
        def _():
            target[...] = jnp.zeros_like(target)
            copy_to(source, source, i_send.at[index], i_recv.at[index], sibling).wait_send()

        @pl.when(owner)
        def _():
            image_local(index, 0).wait()
            ref = source.at[0:5]
            copy_to(ref, ref, i_send.at[index], i_recv.at[index], sibling).wait_send()
            arrived(target.at[0 : 7 * 96, :], i_send.at[index], i_recv.at[index])

    def grad_root(unit):
        return active if UNITS[unit][1] == 0 else w

    def grad_view(unit, rows, side, part=None):
        return grad_root(unit).at[UNITS[unit][0], rows, cols_of(unit, side, part)]

    def reduce_core(unit):
        layer, _start, width, _first, _rows = UNITS[unit]
        root = grad_root(unit)
        for index, side in enumerate((1 - dp, dp)):
            push(
                grad_view(unit, rows_of(side), 1 - core),
                core_buf[unit].at[index],
                rc_send.at[unit],
                rc_recv.at[unit, index],
                sibling,
            )
        sent(reduces, lambda: root.at[layer, 0:D, 0:width], rc_send, unit)

    def reduce_y(unit):
        layer, _start, width, first, _rows = UNITS[unit]
        arrived(core_buf[unit].at[0], rc_send.at[unit], rc_recv.at[unit, 0])

        def add(block, carried):
            ref = grad_view(unit, rows_at((1 - dp) * 4 + block), core)
            ref[...] = (ref[...].astype(F32) + core_buf[unit][0, rows_at(block), :].astype(F32)).astype(BF)
            return carried

        lax.fori_loop(0, 4, add, 0)
        for part, cols in enumerate((slice(0, first), slice(first, width))):
            push(
                grad_view(unit, rows_of(1 - dp), core, part),
                y_buf[unit].at[:, cols],
                ry_send.at[unit],
                ry_recv.at[unit],
                device(1 - dp, z, (y, 1 - y)[part], x, core),
            )
        sent(reduces, lambda: y_buf[unit], ry_send, unit)

    def reduce_z(unit):
        layer, _start, width, first, _rows = UNITS[unit]
        arrived(core_buf[unit].at[1], rc_send.at[unit], rc_recv.at[unit, 1])
        arrived(y_buf[unit], ry_send.at[unit], ry_recv.at[unit])
        for turn in (1, 2, 3, 0):
            block = turned(z, turn, 4)
            ref = grad_view(unit, rows_at(dp * 4 + block), core)
            total = (
                ref[...].astype(F32)
                + core_buf[unit][1, rows_at(block), :].astype(F32)
                + y_buf[unit][rows_at(block), :].astype(F32)
            )
            ref[...] = total.astype(BF)
            if turn:
                push(
                    ref,
                    z_buf[unit].at[turn - 1],
                    rz_send.at[unit],
                    rz_recv.at[unit],
                    device(dp, block, y, x, core),
                )
        sent(reduces, lambda: z_buf[unit], rz_send, unit)

    def reduce_direct(unit):
        layer, _start, width, _first, _rows = UNITS[unit]
        for index in range(2):
            arrived(core_buf[unit].at[index], rc_send.at[unit], rc_recv.at[unit, index])
        for turn in (1, 2, 3, 4, 5, 6, 7, 0):
            to_dp, to_z = turned(dp, turn // 4, 2), turned(z, turn % 4, 4)
            ref = grad_view(unit, rows_at(to_dp * 4 + to_z), core)
            total = ref[...].astype(F32) + core_buf[unit][1 - turn // 4, rows_at(to_z), :].astype(F32)
            ref[...] = total.astype(BF)
            if turn:
                push(
                    ref,
                    z_buf[unit].at[turn - 1],
                    rz_send.at[unit],
                    rz_recv.at[unit],
                    device(to_dp, to_z, y, x, core),
                )
        sent(reduces, lambda: z_buf[unit], rz_send, unit)

    def reduce_slab(unit):
        layer, _start, width, _first, (begin, end) = UNITS[unit]
        total = grad_view(unit, rows_at(dp * 4 + z), core)[...].astype(F32)
        arrived(z_buf[unit], rz_send.at[unit], rz_recv.at[unit])
        for turn in range(1, 8 if unit == 0 else 4):
            total = total + z_buf[unit][turn - 1].astype(F32)
        low = total.astype(BF)
        for group in range((end - begin) // 16):
            parts = [
                low[:, 128 * chunk : 128 * chunk + 128]
                if chunk < width // 128
                else jnp.zeros((ROWS, 128), BF)
                for chunk in range(4 * group, 4 * group + 4)
            ]
            tall = dot_tn(onehot[...], jnp.concatenate(parts, axis=0)).astype(BF)
            at = begin + 16 * group
            slabs[layer, :, at : at + 16, :] = tall.reshape(SPLIT, 16, 128)

    def reduce_plane(group):
        layer, begin, end = GROUPS[group]
        for turn in range(1, 16):
            to_y, to_x, to_core = plane_target(turn)
            push(
                slabs.at[layer, to_y * 8 + to_x * 2 + to_core, begin:end, :],
                ends.at[layer, turn, begin:end, :],
                rp_send.at[group],
                rp_recv.at[group],
                device(dp, z, to_y, to_x, to_core),
            )
        sent(reduces, lambda: slabs.at[layer, 1:16, begin:end, :], rp_send, group)

    outs = ((o_qkv, 0, 9), (o_out, 10, 13), (o_up, 13, 25), (o_down, 25, 37))

    def reduce_end(group):
        layer, begin, end = GROUPS[group]
        totals = [slabs[layer, mine, begin:end, :].astype(F32), None]
        arrived(ends.at[layer, 1:16, begin:end, :], rp_send.at[group], rp_recv.at[group])
        for turn in range(1, 16):
            value = ends[layer, turn, begin:end, :].astype(F32)
            side = turn % 2
            totals[side] = value if totals[side] is None else totals[side] + value
        first = core == 0
        halves = (
            jnp.where(first, totals[0], totals[1]),
            jnp.where(first, totals[1], totals[0]),
        )
        for of, start, width, _first, (low, high) in UNITS:
            for chunk in range(width // 64) if of == layer and begin <= low and high <= end else ():
                inner = low - begin + 4 * (chunk % (width // 128))
                rows = halves[chunk // (width // 128)][inner : inner + 3]
                for target, lowest, highest in outs:
                    if lowest <= start // 128 + chunk < highest:
                        at = 128 * (start // 128 + chunk - lowest)
                        target[:, layer, at : at + 128] = rows

    def misc_out(layer, total):
        tall_sums[...] = jnp.concatenate([total, jnp.zeros((120, D), F32)], axis=0).T
        at = lax.broadcasted_iota(jnp.int32, (8, 128), 0)
        rows = jnp.zeros((8, 128), F32)
        for feature in range(3):
            line = tall_sums[pl.ds(3 * (dp * 64 + sp) + feature, 1), :]
            o_biases[feature, layer : layer + 1, :] = line[:, 2:8]
            rows = jnp.where(at == feature, line, rows)
        wide = jnp.concatenate([rows, jnp.zeros((120, 128), F32)], axis=0).T
        o_gains[layer] = wide[0:2, 0:3]

    def early_sum(stage):
        def send(source, target, where):
            push(source, target, h_send.at[stage], h_recv.at[stage], where)

        def wait(ref):
            arrived(ref, h_send.at[stage - 1], h_recv.at[stage - 1])

        if stage == 0:
            for layer in range(LAYERS):
                early[3 * layer : 3 * layer + 3, :] = hid_sums[layer]
            early[8:16, 0:D] = row_sums[1]
            send(early, h_core, sibling)
            sent(reduces, lambda: early, h_send, 0)
        elif stage == 1:
            wait(h_core)
            h_sum[0] = early[...] + h_core[...]
            send(h_sum.at[0], h_y, device(1 - dp, z, y, x, core))
            sent(reduces, lambda: early, h_send, 1)
        elif stage == 2:
            wait(h_y)
            h_sum[1] = h_sum[0] + h_y[...]
            for turn in range(1, 4):
                send(h_sum.at[1], h_z.at[turn - 1], device(dp, turned(z, turn, 4), y, x, core))
            sent(reduces, lambda: h_z, h_send, 2)
        elif stage == 3:
            wait(h_z)
            h_sum[2] = h_sum[1] + h_z[0] + h_z[1] + h_z[2]
            for turn in range(1, 8):
                where = device(dp, z, turned(y, turn // 4, 2), turned(x, turn % 4, 4), core)
                send(h_sum.at[2], h_p.at[turn], where)
            sent(reduces, lambda: h_p.at[1:8], h_send, 3)
        else:
            wait(h_p.at[1:8])
            total = h_sum[2]
            for turn in range(1, 8):
                total = total + h_p[turn]
            for layer in range(LAYERS):
                for chunk in range(FF // FC):
                    hid[layer, :, FC * chunk : FC * chunk + FC] = total[
                        3 * layer + chunk : 3 * layer + chunk + 1
                    ]
            for layer in range(LAYERS):
                share = pl.ds(pl.multiple_of(dp * (FF // 2), 128), FF // 2)
                o_hid[layer : layer + 1, :] = hid[layer, :, share]
            misc_out(1, total[8:16, 0:D])

    def late_sum(stage):
        if stage == 0:
            late[...] = row_sums[0]
            for turn in range(1, 16):
                where = device(dp, z, *plane_target(turn))
                push(late, l_plane.at[turn], l_send.at[0], l_recv.at[0], where)
            sent(reduces, lambda: l_plane.at[1:16], l_send, 0)
        elif stage == 1:
            arrived(l_plane.at[1:16], l_send.at[0], l_recv.at[0])
            total = late[...]
            for turn in range(1, 16):
                total = total + l_plane[turn]
            l_sum[...] = total
            for turn in range(1, 8):
                where = device(turned(dp, turn // 4, 2), turned(z, turn % 4, 4), y, x, core)
                push(l_sum, l_far.at[turn], l_send.at[1], l_recv.at[1], where)
            sent(reduces, lambda: l_far.at[1:8], l_send, 1)
        else:
            arrived(l_far.at[1:8], l_send.at[1], l_recv.at[1])
            total = l_sum[...]
            for turn in range(1, 8):
                total = total + l_far[turn]
            misc_out(0, total)

    backs = ((act, act_out), (igrad, igrad_out))

    def back_copy(index, home):
        source, target = backs[index]
        return copy_to(
            source.at[96 * home : 96 * home + 96, :],
            target.at[entry_mine],
            e_send.at[index],
            e_recv.at[index],
            device(dp, z, y, home // 2, home % 2),
        )

    def back_local(index, home):
        source, target = backs[index]
        return pltpu.make_async_copy(
            source.at[96 * home : 96 * home + 96, :], target.at[entry_mine], e_local.at[index]
        )

    def back_send(index, first, last):
        for home in range(first, last):

            @pl.when(jnp.logical_and(owner, position != home))
            def _():
                back_copy(index, home).start()

            @pl.when(jnp.logical_and(owner, position == home))
            def _():
                back_local(index, home).start()

    def back_arrive(index):
        source, target = backs[index]

        @pl.when(owner)
        def _():
            back_local(index, 0).wait()
            ref = source.at[0 : 7 * 96, :]
            copy_to(ref, ref, e_send.at[index], e_recv.at[index], sibling).wait_send()
            arrived(target.at[0:5], e_send.at[index], e_recv.at[index])

        @pl.when(jnp.logical_not(owner))
        def _():
            arrived(target, e_send.at[index], e_recv.at[index])

    length = lengths[jnp.minimum(entry_mine, 5), lax.div(dp * 64 + sp, 8)]
    (
        project, attend, feed, turn_back, unfeed, feed_grads, unproject_out, unattend, qkv_grads, unproject,
    ) = encoder(
        length, w, carry, inputs, cot, act, igrad, hid, hid_sums, row_sums,
        mids, qkv, probs_even, probs_odd, invs, att, att_low, active, slope, low_a, low_b, dqkv, trans, trans_b, prm,
    )

    def run(layer, *steps):
        for of in range(LAYERS):
            chosen = [step for step in steps if step[0] == of]
            if chosen:

                @pl.when(layer == of)
                def _():
                    for _of, function, *arguments in chosen:
                        function(*arguments)

    def pairs(body, layer, hooks):
        def one(pair, carried):
            body(layer, pair)
            for at, of, function, *arguments in hooks:

                @pl.when(jnp.logical_and(pair == at, layer == of))
                def _():
                    function(*arguments)

            return carried

        lax.fori_loop(0, PAIRS, one, 0)

    def hidden_arrive():
        arrived(hid_all.at[1 - dp], b_send.at[0], b_recv.at[0])
        for side in range(2):
            for layer in range(LAYERS):
                hid[layer, :, side * (FF // 2) : (side + 1) * (FF // 2)] = hid_all[side, layer : layer + 1, :]

    slab_send(0)
    image_send(0)
    slab_send(1)
    slab_build_layer(1)
    hid_all[dp] = p_hid[...].astype(F32)
    push(hid_all.at[dp], hid_all.at[dp], b_send.at[0], b_recv.at[0], device(1 - dp, z, y, x, core))
    sent(gathers, lambda: hid_all.at[0], b_send, 0)
    onehot[...] = spread_matrix()
    invs[...] = jnp.zeros_like(invs)
    hid_sums[...] = jnp.zeros_like(hid_sums)
    row_sums[...] = jnp.zeros_like(row_sums)
    early[...] = jnp.zeros_like(early)
    slab_arrive(0)
    block_build(0)
    slab_send(2)
    slab_arrive(1)
    block_build(1)
    block_build(2)
    gather_direct(0)
    gather_z(1)
    slab_arrive(2)
    block_build(3)
    block_build(4)
    image_arrive(0)
    carry[...] = img[...].astype(F32)
    gather_z(2)
    gather_end(0)

    def forward(layer, carried):
        project(layer)
        run(layer, (0, gather_y, 1))
        pairs(
            attend,
            layer,
            ((0, 0, gather_z, 3), (0, 0, image_send, 1), (1, 0, gather_y, 2), (1, 1, gather_y, 4)),
        )
        run(
            layer,
            (0, gather_z, 4),
            (0, gather_y, 3),
            (0, hidden_arrive),
            (0, gather_end, 1),
            (0, gather_end, 2),
            (1, gather_end, 4),
        )
        feed(layer)
        run(layer, (0, gather_end, 3))
        return carried

    lax.fori_loop(0, LAYERS, forward, 0)
    back_send(0, 0, 8)
    image_arrive(1)
    turn_back()
    all_sent(gathers)

    def backward(step, carried):
        layer = LAYERS - 1 - step
        unfeed(layer)
        run(layer, (0, early_sum, 0), (0, reduce_z, 4), (0, reduce_y, 3))
        feed_grads(layer)
        run(layer, (0, reduce_core, 2))
        unproject_out(layer)
        run(
            layer,
            (1, reduce_core, 4),
            (0, reduce_core, 1),
            (0, early_sum, 1),
            (0, reduce_z, 3),
            (0, reduce_y, 2),
        )
        pairs(
            unattend,
            layer,
            (
                (0, 0, reduce_y, 1),
                (1, 0, early_sum, 2),
                (1, 0, reduce_slab, 4),
                (1, 0, reduce_z, 2),
                (1, 1, reduce_y, 4),
                (2, 0, reduce_z, 1),
            ),
        )
        run(layer, (0, reduce_slab, 3), (0, reduce_plane, 2), (0, early_sum, 3))
        qkv_grads(layer)
        run(layer, (1, reduce_core, 3), (0, reduce_core, 0))
        unproject(layer, lambda: run(layer, (0, back_send, 1, 0, 4), (0, reduce_direct, 0)))
        return carried

    lax.fori_loop(0, LAYERS, backward, 0)
    late_sum(0)
    back_send(1, 4, 8)
    reduce_slab(2)
    reduce_slab(1)
    reduce_plane(1)
    early_sum(4)
    late_sum(1)
    reduce_slab(0)
    reduce_plane(0)
    reduce_end(2)
    reduce_end(1)
    late_sum(2)
    for index in range(2):
        back_arrive(index)
    reduce_end(0)
    all_sent(reduces)


def finish_kernel(
    i_qkv, i_out, i_up, i_down, i_gains, i_biases, i_hid, i_act, i_igrad,
    act, igrad, g_qkv, g_out, g_up, g_down, g_gains, g_biases, g_hid,
):
    act[...] = i_act[...].astype(F32)
    igrad[...] = i_igrad[...].astype(F32)
    for source, target in (
        (i_qkv, g_qkv),
        (i_out, g_out),
        (i_up, g_up),
        (i_down, g_down),
        (i_gains, g_gains),
        (i_biases, g_biases),
        (i_hid, g_hid),
    ):
        target[...] = source[...]


def local(acts, cotangent, lengths, w_qkv, w_out, w_up, w_down, gains, biases, hidden_bias):
    swap = lambda array: array.transpose(1, 0, 2)
    vmem = pl.BlockSpec(memory_space=pltpu.VMEM)
    any_space = pl.BlockSpec(memory_space=pl.ANY)
    shape = jax.ShapeDtypeStruct
    buffer = pltpu.VMEM
    dma = pltpu.SemaphoreType.DMA
    pair = lambda *dims: [dma(dims), dma(dims)]
    results = pl.pallas_call(
        kernel,
        out_shape=(
            shape((3, LAYERS, 3 * D), F32),
            shape((3, LAYERS, D), F32),
            shape((3, LAYERS, FF), F32),
            shape((3, LAYERS, FF), F32),
            shape((LAYERS, 2, 3), F32),
            shape((3, LAYERS, 6), F32),
            shape((LAYERS, FF // 2), F32),
            shape((6, 96, D), BF),
            shape((6, 96, D), BF),
        ),
        in_specs=[pl.BlockSpec(memory_space=pltpu.SMEM), any_space, any_space] + [vmem] * 7,
        out_specs=(vmem,) * 7 + (any_space,) * 2,
        scratch_shapes=[
            buffer((LAYERS, D, WIDE), BF),
            buffer((TOK, D), F32),
            buffer((LAYERS, TOK, D), F32),
            buffer((TOK, D), BF),
            buffer((TOK, D), BF),
            buffer((TOK, D), BF),
            buffer((4 * ROWS, 256), BF),
            buffer((SLAB, 128), F32),
            buffer((2, LAYERS, FF // 2), F32),
            buffer((LAYERS, 1, FF), F32),
            buffer((LAYERS, 3, FC), F32),
            buffer((LAYERS, 8, D), F32),
            buffer((16, FC), F32),
            buffer((8, D), F32),
            buffer((D, 128), F32),
            *compute_scratch(),
            buffer((LAYERS, 2, SLAB, 128), BF),
            buffer((LAYERS, SPLIT, SLAB, 128), BF),
            buffer((LAYERS, SPLIT, SLAB, 128), BF),
            buffer((LAYERS, SPLIT, SLAB, 128), BF),
            buffer((16, FC), F32),
            buffer((16, FC), F32),
            buffer((3, 16, FC), F32),
            buffer((8, 16, FC), F32),
            buffer((3, 16, FC), F32),
            buffer((16, 8, D), F32),
            buffer((8, 8, D), F32),
            buffer((8, D), F32),
        ]
        + pair(len(GROUPS))
        + pair(COUNT)
        + pair(COUNT)
        + pair(COUNT)
        + [dma((2,)), dma((2,)), dma((2,)), dma((1,)), dma((1,))]
        + [dma((COUNT,)), dma((COUNT, 2))]
        + pair(COUNT)
        + pair(COUNT)
        + pair(len(GROUPS))
        + [dma((2,)), dma((2,)), dma((2,))]
        + pair(4)
        + pair(2)
        + [buffer((2, 4 * ROWS, unit[2]), BF) for unit in UNITS]
        + [buffer((4 * ROWS if index else 16, unit[2]), BF) for index, unit in enumerate(UNITS)]
        + [buffer((3 if index else 7, ROWS, unit[2]), BF) for index, unit in enumerate(UNITS)],
        compiler_params=pltpu.CompilerParams(
            collective_id=0, has_side_effects=True, vmem_limit_bytes=63 * MIB
        ),
        name="encoder",
    )(
        lengths, acts, cotangent, swap(w_qkv), swap(w_out), swap(w_up), swap(w_down),
        gains.transpose(0, 2, 1), swap(biases), hidden_bias,
    )
    act, igrad, g_qkv, g_out, g_up, g_down, g_gains, g_biases, g_hid = pl.pallas_call(
        finish_kernel,
        out_shape=(
            shape((6, 96, D), F32),
            shape((6, 96, D), F32),
            shape((3, LAYERS, 3 * D), F32),
            shape((3, LAYERS, D), F32),
            shape((3, LAYERS, FF), F32),
            shape((3, LAYERS, FF), F32),
            shape((LAYERS, 2, 3), F32),
            shape((3, LAYERS, 6), F32),
            shape((LAYERS, FF // 2), F32),
        ),
        in_specs=[vmem] * 9,
        out_specs=(vmem,) * 9,
        name="finish",
    )(*results)
    return (
        act,
        igrad,
        swap(g_qkv),
        swap(g_out),
        swap(g_up),
        swap(g_down),
        g_gains.transpose(0, 2, 1),
        swap(g_biases),
        g_hid,
    )


def solution(mesh):
    split = P(None, ("dp", "sp"), None)
    return jax.shard_map(
        local,
        mesh=mesh,
        in_specs=(split, split, P(), split, split, split, split, split, split, P(None, "dp")),
        out_specs=(split,) * 8 + (P(None, "dp"),),
        check_vma=False,
    )
```
